128 devices in a mesh: node: 16 (over z, y), local: 8 (over x, core).
Axes of the slice: x: 4, y: 4, z: 4, core: 2. Of those that a mesh axis runs over, the one named last changes fastest.
Arguments:
- hidden: bfloat16 [16384, 3584], P(('node', 'local')), may hold values from -6 to 6
- latent_weight: bfloat16 [3584, 576], P('node'), may hold values from -0.09375 to 0.09375
- latent_gain: float32 [512], replicated, may hold values from 0.1 to 1.9
- queries: bfloat16 [16384, 12288], P(('node', 'local')), may hold values from -200 to 200
- kv_weight: bfloat16 [512, 16384], P('node', 'local'), may hold values from -0.25 to 0.25
- expert_ids: int32 [16384, 8], P(('node', 'local')), may hold values from 0 to 255, as said below
- route_weights: float32 [16384, 8], P(('node', 'local')), may hold values from 0.05 to 0.6
- gate_proj: bfloat16 [128, 3584, 512], P(('node', 'local')), may hold values from -0.09375 to 0.09375
- up_proj: bfloat16 [128, 3584, 512], P(('node', 'local')), may hold values from -0.09375 to 0.09375
- down_proj: bfloat16 [128, 512, 3584], P(('node', 'local')), may hold values from -0.1875 to 0.1875
Outputs:
- attention: bfloat16 [16384, 8192], P(('node', 'local'))
- routed: bfloat16 [16384, 3584], P(('node', 'local'))
The draws below stay inside these ranges and needn't reach their ends.
Inputs may be any that keep to these rules, and one draw needn't show every extreme that they name: `expert_ids`: each row names 8 different experts, all of them in at most 4 of the 8 groups of 32 consecutive expert numbers.
All inputs are finite; a program needn't handle non-finite values.
Results may differ from the reference program's by a relative error of at most 0.014.
The reference program's roundings to bfloat16 on the way count: a program that leaves them out, or rounds other values in their place, can miss the bound.
Values may be sent and summed in bfloat16 or wider, within the bound.
No kernel may reach another device: no remote copies, remote signals or barrier semaphores. Data moves between devices by JAX's collectives and lax.ppermute only.
A program may use at most 128 MiB of HBM per device.

```python
import math
import jax
import jax.numpy as jnp
from jax import lax

D = 3584
HEADS = 64
NOPE = 128
ROPE = 64
VDIM = 128
LAT = 512
EXPERTS = 256
GROUPS = 8
TOPK = 8
FF_E = 1024
TOK_DEV = 128
L = 1024
TOKENS = 16384
FLIGHT = 64
STRIDE = 4
CAP = 8
N_NODE = 16
N_LOCAL = 8


def draw_queries(key, part):
    key = jax.random.fold_in(key, 11)
    shape = (TOKENS, HEADS * (NOPE + ROPE))
    return jax.random.normal(key, shape, jnp.float32).astype(jnp.bfloat16)


def draw_expert_ids(key, part):
    key = jax.random.fold_in(key, 5)
    group_key, bias_key, expert_key, pick_key = jax.random.split(key, 4)
    per_group = EXPERTS // GROUPS
    group_bias = jax.random.randint(bias_key, (GROUPS,), 0, 4) * 32768
    group_scores = jax.random.randint(group_key, (TOKENS, GROUPS), 0, 65536) + group_bias[None, :]
    group_scores = group_scores * GROUPS + jnp.arange(GROUPS, dtype=jnp.int32)[None, :]
    chosen = lax.top_k(group_scores, 4)[1]
    expert_group = jnp.arange(EXPERTS, dtype=jnp.int32) // per_group
    allowed = jnp.any(chosen[:, :, None] == expert_group[None, None, :], axis=1)
    popularity = jax.random.randint(expert_key, (EXPERTS,), 0, 8)
    popularity = popularity * popularity * 2048
    scores = jax.random.randint(pick_key, (TOKENS, EXPERTS), 0, 65536) + popularity[None, :]
    scores = jnp.where(allowed, scores, -1) * EXPERTS + jnp.arange(EXPERTS, dtype=jnp.int32)[None, :]
    return lax.top_k(scores, TOPK)[1].astype(jnp.int32)


def steps_of(rng, shape, pieces, least, top_value):
    factor_of, own = 1.0, jax.random.fold_in(rng, 6)
    for axis_at, blocks in pieces:
        steps = jnp.exp(jax.random.uniform(jax.random.fold_in(own, axis_at), (blocks,), jnp.float32, least / len(pieces), top_value / len(pieces)))
        factor_of = factor_of * jnp.repeat(steps, shape[axis_at] // blocks).reshape([-1 if axis == axis_at else 1 for axis in range(len(shape))])
    return factor_of


def centred(key, extent, deviation, reach, pieces=(), held_as=jnp.bfloat16):
    loudness = steps_of(key, extent, pieces, -0.22, 0.18) if pieces else 1.0
    entries = jax.random.normal(key, extent, jnp.float32) * deviation * loudness
    return jnp.minimum(jnp.maximum(entries, -reach), reach).astype(held_as)


def setup_inputs(seed: int = 0) -> dict:
    arg_keys = jax.random.split(jax.random.key(seed), 11)
    hidden = centred(arg_keys[0], (TOKENS, D), 1.0, 6.0, ((0, 128),))
    latent_weight = centred(arg_keys[1], (D, LAT + ROPE), D ** -0.5, 0.09375, ((0, 16),))
    latent_gain = jnp.clip(1.0 + 0.18 * jax.random.normal(arg_keys[2], (LAT,), jnp.float32), 0.1, 1.9)
    queries = draw_queries(jax.random.fold_in(arg_keys[10], 71), 0)
    kv_weight = centred(arg_keys[4], (LAT, HEADS * (NOPE + VDIM)), LAT ** -0.5, 0.25, ((0, 16), (1, 8)))
    expert_ids = draw_expert_ids(jax.random.fold_in(arg_keys[10], 71), 0)
    route_weights = jnp.clip(0.05 + 0.55 * jax.random.uniform(arg_keys[6], (TOKENS, TOPK), jnp.float32) ** steps_of(arg_keys[6], (TOKENS, TOPK), ((0, 128),), -0.2, 0.2), 0.05, 0.6)
    gate_proj = centred(arg_keys[7], (2 * FLIGHT, D, FF_E // 2), D ** -0.5, 0.09375, ((0, 128),))
    up_proj = centred(arg_keys[8], (2 * FLIGHT, D, FF_E // 2), D ** -0.5, 0.09375, ((0, 128),))
    down_proj = centred(arg_keys[9], (2 * FLIGHT, FF_E // 2, D), FF_E ** -0.5, 0.1875, ((0, 128),))
    return dict(hidden=hidden, latent_weight=latent_weight, latent_gain=latent_gain, queries=queries, kv_weight=kv_weight, expert_ids=expert_ids, route_weights=route_weights, gate_proj=gate_proj, up_proj=up_proj, down_proj=down_proj)


def normalize(columns, latent_gain):
    mean_square = lax.optimization_barrier(jnp.mean(columns * columns, axis=1, keepdims=True))
    return (columns * lax.rsqrt(mean_square + 1e-06) * latent_gain[None, :]).astype(jnp.bfloat16)

def rotate_keys(rope_part, position):
    half_width = ROPE // 2
    freqs = 10000.0 ** (-2.0 * jnp.arange(half_width, dtype=jnp.float32) / ROPE)
    angles = position.astype(jnp.float32)[:, None] * freqs[None, :]
    cosine = jnp.cos(angles)
    sine = jnp.sin(angles)
    first_half = rope_part[:, :half_width]
    second_half = rope_part[:, half_width:]
    return jnp.concatenate([first_half * cosine - second_half * sine, second_half * cosine + first_half * sine], axis=1)

def attend_head(query_rows, keyval, keys_rope):
    length = query_rows.shape[0]
    q_block = min(length, 512)
    keys_nope = keyval[:, :NOPE]
    values = keyval[:, NOPE:]
    scale = 1.0 / math.sqrt(NOPE + ROPE)

    def one_block(block_index):
        offset = block_index * q_block
        block_rows = lax.dynamic_slice_in_dim(query_rows, offset, q_block, 0)
        scores = jnp.dot(block_rows[:, :NOPE], keys_nope.T, preferred_element_type=jnp.float32)
        scores = scores + jnp.dot(block_rows[:, NOPE:], keys_rope.T, preferred_element_type=jnp.float32)
        scores = scores * scale
        query_pos = offset + jnp.arange(q_block, dtype=jnp.int32)[:, None]
        key_pos = jnp.arange(length, dtype=jnp.int32)[None, :]
        scores = jnp.where(key_pos <= query_pos, scores, -1e+30)
        row_max = lax.optimization_barrier(jnp.max(scores, axis=1, keepdims=True))
        weights = jnp.exp(scores - row_max)
        probs = (weights / lax.optimization_barrier(jnp.sum(weights, axis=1, keepdims=True))).astype(jnp.bfloat16)
        return jnp.dot(probs, values, preferred_element_type=jnp.float32).astype(jnp.bfloat16)
    blocks = lax.map(one_block, jnp.arange(length // q_block, dtype=jnp.int32))
    return blocks.reshape(length, values.shape[1])

def reference(hidden, latent_weight, latent_gain, queries, kv_weight, expert_ids, route_weights, gate_proj, up_proj, down_proj):
    latent = jnp.dot(hidden, latent_weight, preferred_element_type=jnp.float32)
    compressed = normalize(latent[:, :LAT], latent_gain)
    position = jnp.arange(TOKENS, dtype=jnp.int32) % L
    rope_keys = rotate_keys(latent[:, LAT:], position).astype(jnp.bfloat16)

    def one_sequence(packed):
        seq_queries, seq_latent, seq_rope = packed
        keyval = jnp.dot(seq_latent, kv_weight, preferred_element_type=jnp.float32).astype(jnp.bfloat16)
        head_queries = seq_queries.reshape(L, HEADS, NOPE + ROPE).transpose(1, 0, 2)
        head_keyval = keyval.reshape(L, HEADS, NOPE + VDIM).transpose(1, 0, 2)
        outputs = lax.map(lambda head_pair: attend_head(head_pair[0], head_pair[1], seq_rope), (head_queries, head_keyval))
        return outputs.transpose(1, 0, 2).reshape(L, HEADS * VDIM)
    sequences = TOKENS // L
    attention = lax.map(one_sequence, (queries.reshape(sequences, L, HEADS * (NOPE + ROPE)), compressed.reshape(sequences, L, LAT), rope_keys.reshape(sequences, L, ROPE)))
    attention = attention.reshape(TOKENS, HEADS * VDIM)
    devices = N_NODE * N_LOCAL
    routes_flat = expert_ids.reshape(devices, TOK_DEV * TOPK)
    in_flight = routes_flat % STRIDE == 0
    target = routes_flat // STRIDE
    onehot = ((target[:, :, None] == jnp.arange(FLIGHT, dtype=jnp.int32)[None, None, :]) & in_flight[:, :, None]).astype(jnp.int32)
    slot_index = lax.optimization_barrier(jnp.sum((jnp.cumsum(onehot, axis=1) - onehot) * onehot, axis=2))
    kept_mask = in_flight & (slot_index < CAP)
    block_ids = jnp.arange(devices, dtype=jnp.int32)[:, None]
    dump_slot = FLIGHT * devices * CAP
    place_index = jnp.where(kept_mask, target * (devices * CAP) + block_ids * CAP + slot_index, dump_slot)
    token_index = block_ids * TOK_DEV + jnp.arange(TOK_DEV * TOPK, dtype=jnp.int32)[None, :] // TOPK
    row_table = jnp.full((dump_slot + 1,), TOKENS, jnp.int32).at[place_index.reshape(-1)].set(token_index.reshape(-1))[:dump_slot]
    padded = jnp.concatenate([hidden, jnp.zeros((1, D), jnp.bfloat16)], axis=0)
    half_width = FF_E // 2

    def run_expert(packed):
        expert_table, gates, ups, downs = packed
        row_block = padded[expert_table]
        halves = []
        for core_half in range(2):
            gate = jnp.dot(row_block, gates[core_half], preferred_element_type=jnp.float32)
            upper = jnp.dot(row_block, ups[core_half], preferred_element_type=jnp.float32)
            inner = (jax.nn.silu(gate) * upper).astype(jnp.bfloat16)
            halves.append(jnp.dot(inner, downs[core_half], preferred_element_type=jnp.float32).astype(jnp.bfloat16))
        return (halves[0].astype(jnp.float32) + halves[1].astype(jnp.float32)).astype(jnp.bfloat16)
    results = lax.map(run_expert, (row_table.reshape(FLIGHT, devices * CAP), gate_proj.reshape(FLIGHT, 2, D, half_width), up_proj.reshape(FLIGHT, 2, D, half_width), down_proj.reshape(FLIGHT, 2, half_width, D)))
    results = jnp.concatenate([results.reshape(FLIGHT * devices * CAP, D), jnp.zeros((1, D), jnp.bfloat16)], axis=0)
    route_index = place_index.reshape(TOKENS, TOPK)
    routed = jnp.zeros((TOKENS, D), jnp.float32)
    for column in range(TOPK):
        routed = routed + route_weights[:, column:column + 1] * results[route_index[:, column]].astype(jnp.float32)
    return (attention, routed.astype(jnp.bfloat16))
```

```python
import functools
import math

import jax
import jax.numpy as jnp
from jax import lax
from jax.experimental import pallas as pl
from jax.experimental.pallas import tpu as pltpu
from jax.sharding import Mesh
from jax.sharding import PartitionSpec as P

NOPE = 128
ROPE = 64
VDIM = 128
LAT = 512
EXPERTS = 256
TOPK = 8
CAP = 8
HEAD = NOPE + ROPE
KV = NOPE + VDIM
CHIPS = ("z", "y", "x")
ALL = ("z", "y", "x", "c")
BF16 = jnp.bfloat16
F32 = jnp.float32
MIB = 1 << 20


def call(kernel, **options):
    limit = options.pop("vmem", 32)
    flops, moved = options.pop("cost")
    return pl.pallas_call(
        kernel,
        compiler_params=pltpu.CompilerParams(vmem_limit_bytes=limit * MIB),
        cost_estimate=pl.CostEstimate(flops=flops, bytes_accessed=moved, transcendentals=0),
        **options,
    )


def dispatch_kernel(ids_ref, weights_ref, hidden_ref, rows_ref, gate_ref, pick):
    slots, tokens = pick.shape

    @pl.when(pl.program_id(0) == 0)
    def _():
        row = lax.broadcasted_iota(jnp.int32, (slots, tokens), 0)
        number = (row // CAP) * (EXPERTS * CAP // slots)
        named = jnp.zeros((slots, tokens), F32)
        weight = jnp.zeros((slots, tokens), F32)
        for k in range(TOPK):
            here = ids_ref[k : k + 1, :] == number
            named = jnp.where(here, 1.0, named)
            weight = jnp.where(here, weights_ref[k : k + 1, :], weight)
        before = lax.broadcasted_iota(jnp.int32, (tokens, tokens), 0) < lax.broadcasted_iota(
            jnp.int32, (tokens, tokens), 1
        )
        earlier = jnp.dot(
            named.astype(BF16), before.astype(F32).astype(BF16), preferred_element_type=F32
        )
        kept = (named > 0.5) & (earlier.astype(jnp.int32) == row % CAP)
        pick[...] = jnp.where(kept, 1.0, 0.0).astype(BF16)
        gate_ref[...] = jnp.where(kept, weight, 0.0)

    rows_ref[...] = jnp.dot(pick[...], hidden_ref[...], preferred_element_type=F32).astype(BF16)


def dispatch(ids, weights, hidden, slots):
    tokens, width = hidden.shape
    block = 512
    return call(
        dispatch_kernel,
        cost=(2 * slots * tokens * width, 2 * (slots + tokens) * width),
        grid=(width // block,),
        in_specs=[
            pl.BlockSpec((TOPK, tokens), lambda j: (0, 0)),
            pl.BlockSpec((TOPK, tokens), lambda j: (0, 0)),
            pl.BlockSpec((tokens, block), lambda j: (0, j)),
        ],
        out_specs=[
            pl.BlockSpec((slots, block), lambda j: (0, j)),
            pl.BlockSpec((slots, tokens), lambda j: (0, 0)),
        ],
        out_shape=[
            jax.ShapeDtypeStruct((slots, width), BF16),
            jax.ShapeDtypeStruct((slots, tokens), F32),
        ],
        scratch_shapes=[pltpu.VMEM((slots, tokens), BF16)],
    )(ids, weights, hidden)


def combine_kernel(gate_ref, rows_ref, out_ref, terms):
    tokens = out_ref.shape[0]

    @pl.when(pl.program_id(0) == 0)
    def _():
        rest = gate_ref[...]
        for term in range(3):
            part = rest.astype(BF16)
            terms[:, term * tokens : (term + 1) * tokens] = part
            rest = rest - part.astype(F32)

    total = lax.dot_general(
        terms[...], rows_ref[...], (((0,), (0,)), ((), ())), preferred_element_type=F32
    )
    out_ref[...] = (total[:tokens] + total[tokens : 2 * tokens] + total[2 * tokens :]).astype(BF16)


def combine(gate, rows):
    slots, tokens = gate.shape
    width = rows.shape[1]
    block = 512
    return call(
        combine_kernel,
        cost=(6 * slots * tokens * width, 2 * (slots + tokens) * width),
        grid=(width // block,),
        in_specs=[
            pl.BlockSpec((slots, tokens), lambda j: (0, 0)),
            pl.BlockSpec((slots, block), lambda j: (0, j)),
        ],
        out_specs=pl.BlockSpec((tokens, block), lambda j: (0, j)),
        out_shape=jax.ShapeDtypeStruct((tokens, width), BF16),
        scratch_shapes=[pltpu.VMEM((slots, 3 * tokens), BF16)],
    )(gate, rows)


def expert_kernel(
    rows_ref, gate0, up0, down0, gate1, up1, down1, out_ref, inner, *, steps
):
    step = pl.program_id(0)

    def hidden_block(gate_ref, up_ref):
        rows = rows_ref[...]
        gate = jnp.dot(rows, gate_ref[0], preferred_element_type=F32)
        upper = jnp.dot(rows, up_ref[0], preferred_element_type=F32)
        inner[step] = (gate / (1.0 + jnp.exp(-gate)) * upper).astype(BF16)

    pl.when(step < steps)(lambda: hidden_block(gate0, up0))
    pl.when((step >= steps) & (step < 2 * steps))(lambda: hidden_block(gate1, up1))

    @pl.when(step >= 2 * steps)
    def _():
        wide = inner.shape[2]
        total = None
        for half, down in enumerate((down0, down1)):
            partial = None
            for part in range(steps):
                term = jnp.dot(
                    inner[half * steps + part],
                    down[0, part * wide : (part + 1) * wide, :],
                    preferred_element_type=F32,
                )
                partial = term if partial is None else partial + term
            partial = partial.astype(BF16).astype(F32)
            total = partial if total is None else total + partial
        out_ref[...] = total.astype(BF16)


def experts(rows, own, other):
    count, width = rows.shape
    half = own[0].shape[2]
    wide, block = 256, 512
    steps = half // wide
    first = 2 * steps

    def column(start):
        return lambda j: (0, 0, jnp.clip(j - start, 0, steps - 1))

    def late(j):
        return (0, 0, jnp.maximum(j - first, 0))

    specs = []
    for start in (0, steps):
        specs += [
            pl.BlockSpec((1, width, wide), column(start)),
            pl.BlockSpec((1, width, wide), column(start)),
            pl.BlockSpec((1, half, block), late),
        ]
    return call(
        functools.partial(expert_kernel, steps=steps),
        vmem=56,
        cost=(12 * count * width * half, 2 * (2 * count * width + 6 * width * half)),
        grid=(first + width // block,),
        in_specs=[pl.BlockSpec((count, width), lambda j: (0, 0))] + specs,
        out_specs=pl.BlockSpec((count, block), lambda j: (0, jnp.maximum(j - first, 0))),
        out_shape=jax.ShapeDtypeStruct((count, width), BF16),
        scratch_shapes=[pltpu.VMEM((first, count, wide), BF16)],
    )(rows, *own, *other)


def attention_kernel(
    where_ref, latent_ref, kv_ref, mine_ref, other_ref, out_ref, send_ref, bias
):
    tokens = mine_ref.shape[0]
    length = latent_ref.shape[0]
    chips = length // (2 * tokens)

    @pl.when(pl.program_id(0) == 0)
    def _():
        core, chip = where_ref[0], where_ref[1]
        row = lax.broadcasted_iota(jnp.int32, (2 * tokens, length), 0)
        col = lax.broadcasted_iota(jnp.int32, (2 * tokens, length), 1)
        row_core = jnp.where(row < tokens, core, 1 - core)
        row_at = (2 * chip + row_core) * tokens + row % tokens
        block = col // tokens
        col_core = jnp.where(block < chips, core, 1 - core)
        col_chip = (chip + chips - block % chips) % chips
        col_at = (2 * col_chip + col_core) * tokens + col % tokens
        bias[...] = jnp.where(col_at <= row_at, 0.0, -1e30)

    compressed = latent_ref[:, :LAT]
    rope = latent_ref[:, LAT:]
    weight = kv_ref[...].reshape(LAT, 2 * KV)
    keyval = jnp.dot(compressed, weight, preferred_element_type=F32).astype(BF16)
    factor = math.log2(math.e) / math.sqrt(HEAD)
    for head in range(2):
        keys = jnp.concatenate([keyval[:, head * KV : head * KV + NOPE], rope], axis=1)
        values = keyval[:, head * KV + NOPE : (head + 1) * KV]
        span = slice(head * HEAD, (head + 1) * HEAD)
        query = jnp.concatenate([mine_ref[:, span], other_ref[:, span]], axis=0)
        score = lax.dot_general(
            query, keys, (((1,), (1,)), ((), ())), preferred_element_type=F32
        )
        score = score + bias[...]
        top = jnp.max(score, axis=1, keepdims=True)
        weights = jnp.exp2((score - top) * factor)
        inverse = 1.0 / jnp.sum(weights, axis=1, keepdims=True)
        probs = (weights * inverse).astype(BF16)
        result = jnp.dot(probs, values, preferred_element_type=F32).astype(BF16)
        span = slice(head * VDIM, (head + 1) * VDIM)
        out_ref[:, span] = result[:tokens]
        send_ref[:, span] = result[tokens:]


def attend(where, latent, kv_weight, mine, other):
    tokens = mine.shape[0]
    length = latent.shape[0]
    nodes, chips, rows, columns = kv_weight.shape
    pairs = columns // (2 * KV)
    heads = 2 * pairs * chips
    spec = pltpu.PrefetchScalarGridSpec(
        num_scalar_prefetch=1,
        grid=(chips * pairs,),
        in_specs=[
            pl.BlockSpec((length, LAT + ROPE), lambda i, w: (0, 0)),
            pl.BlockSpec((nodes, 1, rows, 2 * KV), lambda i, w: (0, i // pairs, 0, i % pairs)),
            pl.BlockSpec(
                (tokens, 2 * HEAD), lambda i, w: (0, (2 * (i // pairs) + w[0]) * pairs + i % pairs)
            ),
            pl.BlockSpec((tokens, 2 * HEAD), lambda i, w: (0, i)),
        ],
        out_specs=[
            pl.BlockSpec(
                (tokens, 2 * VDIM), lambda i, w: (0, (2 * (i // pairs) + w[0]) * pairs + i % pairs)
            ),
            pl.BlockSpec((tokens, 2 * VDIM), lambda i, w: (0, i)),
        ],
        scratch_shapes=[pltpu.VMEM((2 * tokens, length), F32)],
    )
    flops = 2 * heads * length * (LAT * KV + 2 * tokens * (HEAD + VDIM))
    return call(
        attention_kernel,
        vmem=48,
        cost=(2 * flops, 2 * (LAT * heads * KV + 4 * tokens * heads * HEAD)),
        grid_spec=spec,
        out_shape=[
            jax.ShapeDtypeStruct((tokens, 2 * heads * VDIM), BF16),
            jax.ShapeDtypeStruct((tokens, heads * VDIM), BF16),
        ],
    )(where, latent, kv_weight, mine, other)


def merge_kernel(where_ref, part_ref, whole_ref, out_ref):
    out_ref[...] = part_ref[...]


def merge(where, part, whole, chips):
    tokens, columns = part.shape
    block = columns // chips
    spec = pltpu.PrefetchScalarGridSpec(
        num_scalar_prefetch=1,
        grid=(chips,),
        in_specs=[
            pl.BlockSpec((tokens, block), lambda i, w: (0, i)),
            pl.BlockSpec(memory_space=pl.ANY),
        ],
        out_specs=pl.BlockSpec((tokens, block), lambda i, w: (0, 2 * i + 1 - w[0])),
    )
    return call(
        merge_kernel,
        cost=(0, 4 * tokens * columns),
        grid_spec=spec,
        out_shape=jax.ShapeDtypeStruct(whole.shape, BF16),
        input_output_aliases={2: 0},
    )(where, part, whole)


def normalize(columns, latent_gain):
    mean_square = jnp.mean(columns * columns, axis=1, keepdims=True)
    return (columns * lax.rsqrt(mean_square + 1e-06) * latent_gain[None, :]).astype(BF16)


def rotate_keys(rope_part, position):
    half_width = ROPE // 2
    freqs = 10000.0 ** (-2.0 * jnp.arange(half_width, dtype=F32) / ROPE)
    angles = position.astype(F32)[:, None] * freqs[None, :]
    cosine = jnp.cos(angles)
    sine = jnp.sin(angles)
    first_half = rope_part[:, :half_width]
    second_half = rope_part[:, half_width:]
    return jnp.concatenate(
        [first_half * cosine - second_half * sine, second_half * cosine + first_half * sine], axis=1
    ).astype(BF16)


def swap(array):
    return lax.ppermute(array, "c", [(0, 1), (1, 0)])


def along_x(array, distance):
    size = lax.axis_size("x")
    return lax.ppermute(array, "x", [(i, (i + distance) % size) for i in range(size)])


def exchange(rows):
    return lax.all_to_all(rows, CHIPS, split_axis=0, concat_axis=0, tiled=True)


def shards(
    hidden,
    latent_weight,
    latent_gain,
    queries,
    kv_weight,
    expert_ids,
    route_weights,
    gate_proj,
    up_proj,
    down_proj,
):
    tokens = hidden.shape[0]
    core = lax.axis_index("c")
    chip = lax.axis_index("x")
    chips = lax.axis_size("x")
    nodes = lax.axis_size("z") * lax.axis_size("y")
    where = jnp.stack([core, chip]).astype(jnp.int32)

    slots = nodes * chips * CAP
    rows, gate = dispatch(expert_ids.T, route_weights.T, hidden, slots)
    arrived = exchange(rows)

    own = (gate_proj, up_proj, down_proj)
    other = tuple(swap(array) for array in own)

    portion = lax.all_gather(latent_weight, ("z", "y"), axis=0, tiled=True)
    latent = jnp.dot(hidden, portion, preferred_element_type=F32)
    position = (2 * chip + core) * tokens + jnp.arange(tokens, dtype=jnp.int32)
    mine = jnp.concatenate(
        [normalize(latent[:, :LAT], latent_gain), rotate_keys(latent[:, LAT:], position)], axis=1
    )
    line = jnp.concatenate([mine] + [along_x(mine, d) for d in range(1, chips)], axis=0)
    sequence = jnp.concatenate([line, swap(line)], axis=0)

    kv_rows, kv_columns = kv_weight.shape
    kv_all = lax.all_gather(kv_weight, CHIPS, axis=0, tiled=True)
    kv_all = kv_all.reshape(nodes, chips, kv_rows, kv_columns)

    split = queries.reshape(tokens, chips, 2, -1)
    sent = lax.dynamic_index_in_dim(split, 1 - core, axis=2, keepdims=False)
    other_queries = swap(sent.reshape(tokens, -1))

    results = experts(arrived, own, other)
    sequence, results = lax.optimization_barrier((sequence, results))
    returned = exchange(results)

    whole, send = attend(where, sequence, kv_all, queries, other_queries)
    attention = merge(where, swap(send), whole, chips)
    routed = combine(gate, returned)
    return (attention, routed)


def solution(mesh):
    grid = Mesh(mesh.devices.reshape(4, 4, 4, 2), ALL)
    token = P(ALL, None)
    placed = (
        token,
        P(("z", "y"), None),
        P(),
        token,
        P(("z", "y"), ("x", "c")),
        token,
        token,
        P(ALL, None, None),
        P(ALL, None, None),
        P(ALL, None, None),
    )
    return jax.shard_map(
        shards, mesh=grid, in_specs=placed, out_specs=(token, token), check_vma=False
    )
```

```python
import functools
import math

import jax
import jax.numpy as jnp
from jax import lax
from jax.experimental import pallas as pl
from jax.experimental.pallas import tpu as pltpu
from jax.sharding import Mesh
from jax.sharding import PartitionSpec as P

NOPE = 128
ROPE = 64
VDIM = 128
LAT = 512
EXPERTS = 256
TOPK = 8
CAP = 8
HEAD = NOPE + ROPE
KV = NOPE + VDIM
CHIPS = ("z", "y", "x")
ALL = ("z", "y", "x", "c")
BF16 = jnp.bfloat16
F32 = jnp.float32
MIB = 1 << 20


def call(kernel, **options):
    limit = options.pop("vmem", 32)
    flops, moved = options.pop("cost")
    return pl.pallas_call(
        kernel,
        compiler_params=pltpu.CompilerParams(vmem_limit_bytes=limit * MIB),
        cost_estimate=pl.CostEstimate(flops=flops, bytes_accessed=moved, transcendentals=0),
        **options,
    )


def dispatch_kernel(ids_ref, weights_ref, hidden_ref, rows_ref, gate_ref, pick):
    slots, tokens = pick.shape

    @pl.when(pl.program_id(0) == 0)
    def _():
        row = lax.broadcasted_iota(jnp.int32, (slots, tokens), 0)
        number = (row // CAP) * (EXPERTS * CAP // slots)
        named = jnp.zeros((slots, tokens), F32)
        weight = jnp.zeros((slots, tokens), F32)
        for k in range(TOPK):
            here = ids_ref[k : k + 1, :] == number
            named = jnp.where(here, 1.0, named)
            weight = jnp.where(here, weights_ref[k : k + 1, :], weight)
        before = lax.broadcasted_iota(jnp.int32, (tokens, tokens), 0) < lax.broadcasted_iota(
            jnp.int32, (tokens, tokens), 1
        )
        earlier = jnp.dot(
            named.astype(BF16), before.astype(F32).astype(BF16), preferred_element_type=F32
        )
        kept = (named > 0.5) & (earlier.astype(jnp.int32) == row % CAP)
        pick[...] = jnp.where(kept, 1.0, 0.0).astype(BF16)
        gate_ref[...] = jnp.where(kept, weight, 0.0)

    rows_ref[...] = jnp.dot(pick[...], hidden_ref[...], preferred_element_type=F32).astype(BF16)


def dispatch(ids, weights, hidden, slots):
    tokens, width = hidden.shape
    block = 512
    return call(
        dispatch_kernel,
        cost=(2 * slots * tokens * width, 2 * (slots + tokens) * width),
        grid=(width // block,),
        in_specs=[
            pl.BlockSpec((TOPK, tokens), lambda j: (0, 0)),
            pl.BlockSpec((TOPK, tokens), lambda j: (0, 0)),
            pl.BlockSpec((tokens, block), lambda j: (0, j)),
        ],
        out_specs=[
            pl.BlockSpec((slots, block), lambda j: (0, j)),
            pl.BlockSpec((slots, tokens), lambda j: (0, 0)),
        ],
        out_shape=[
            jax.ShapeDtypeStruct((slots, width), BF16),
            jax.ShapeDtypeStruct((slots, tokens), F32),
        ],
        scratch_shapes=[pltpu.VMEM((slots, tokens), BF16)],
    )(ids, weights, hidden)


def combine_kernel(gate_ref, rows_ref, out_ref, terms):
    tokens = out_ref.shape[0]

    @pl.when(pl.program_id(0) == 0)
    def _():
        rest = gate_ref[...]
        for term in range(3):
            part = rest.astype(BF16)
            terms[:, term * tokens : (term + 1) * tokens] = part
            rest = rest - part.astype(F32)

    total = lax.dot_general(
        terms[...], rows_ref[...], (((0,), (0,)), ((), ())), preferred_element_type=F32
    )
    out_ref[...] = (total[:tokens] + total[tokens : 2 * tokens] + total[2 * tokens :]).astype(BF16)


def combine(gate, rows):
    slots, tokens = gate.shape
    width = rows.shape[1]
    block = 1792
    return call(
        combine_kernel,
        cost=(6 * slots * tokens * width, 2 * (slots + tokens) * width),
        grid=(width // block,),
        in_specs=[
            pl.BlockSpec((slots, tokens), lambda j: (0, 0)),
            pl.BlockSpec((slots, block), lambda j: (0, j)),
        ],
        out_specs=pl.BlockSpec((tokens, block), lambda j: (0, j)),
        out_shape=jax.ShapeDtypeStruct((tokens, width), BF16),
        scratch_shapes=[pltpu.VMEM((slots, 3 * tokens), BF16)],
    )(gate, rows)


def expert_kernel(
    rows_ref, gate0, up0, down0, gate1, up1, down1, out_ref, inner, *, steps
):
    step = pl.program_id(0)

    def hidden_block(gate_ref, up_ref):
        rows = rows_ref[...]
        gate = jnp.dot(rows, gate_ref[0], preferred_element_type=F32)
        upper = jnp.dot(rows, up_ref[0], preferred_element_type=F32)
        inner[step] = (gate / (1.0 + jnp.exp(-gate)) * upper).astype(BF16)

    pl.when(step < steps)(lambda: hidden_block(gate0, up0))
    pl.when((step >= steps) & (step < 2 * steps))(lambda: hidden_block(gate1, up1))

    @pl.when(step >= 2 * steps)
    def _():
        wide = inner.shape[2]
        total = None
        for half, down in enumerate((down0, down1)):
            partial = None
            for part in range(steps):
                term = jnp.dot(
                    inner[half * steps + part],
                    down[0, part * wide : (part + 1) * wide, :],
                    preferred_element_type=F32,
                )
                partial = term if partial is None else partial + term
            partial = partial.astype(BF16).astype(F32)
            total = partial if total is None else total + partial
        out_ref[...] = total.astype(BF16)


def experts(rows, own, other):
    count, width = rows.shape
    half = own[0].shape[2]
    wide, block = 256, 1792
    steps = half // wide
    first = 2 * steps

    def column(start):
        return lambda j: (0, 0, jnp.clip(j - start, 0, steps - 1))

    def late(j):
        return (0, 0, jnp.maximum(j - first, 0))

    specs = []
    for start in (0, steps):
        specs += [
            pl.BlockSpec((1, width, wide), column(start)),
            pl.BlockSpec((1, width, wide), column(start)),
            pl.BlockSpec((1, half, block), late),
        ]
    return call(
        functools.partial(expert_kernel, steps=steps),
        vmem=56,
        cost=(12 * count * width * half, 2 * (2 * count * width + 6 * width * half)),
        grid=(first + width // block,),
        in_specs=[pl.BlockSpec((count, width), lambda j: (0, 0))] + specs,
        out_specs=pl.BlockSpec((count, block), lambda j: (0, jnp.maximum(j - first, 0))),
        out_shape=jax.ShapeDtypeStruct((count, width), BF16),
        scratch_shapes=[pltpu.VMEM((first, count, wide), BF16)],
    )(rows, *own, *other)


def attention_kernel(
    where_ref, latent_ref, kv_ref, mine_ref, other_ref, out_ref, send_ref, bias
):
    tokens = mine_ref.shape[0]
    length = latent_ref.shape[0]
    chips = length // (2 * tokens)

    @pl.when(pl.program_id(0) == 0)
    def _():
        core, chip = where_ref[0], where_ref[1]
        row = lax.broadcasted_iota(jnp.int32, (2 * tokens, length), 0)
        col = lax.broadcasted_iota(jnp.int32, (2 * tokens, length), 1)
        row_core = jnp.where(row < tokens, core, 1 - core)
        row_at = (2 * chip + row_core) * tokens + row % tokens
        block = col // tokens
        col_core = jnp.where(block < chips, core, 1 - core)
        col_chip = (chip + chips - block % chips) % chips
        col_at = (2 * col_chip + col_core) * tokens + col % tokens
        bias[...] = jnp.where(col_at <= row_at, 0.0, -1e30)

    compressed = latent_ref[:, :LAT]
    rope = latent_ref[:, LAT:]
    weight = kv_ref[...].reshape(LAT, 2 * KV)
    keyval = jnp.dot(compressed, weight, preferred_element_type=F32).astype(BF16)
    factor = math.log2(math.e) / math.sqrt(HEAD)
    for head in range(2):
        keys = jnp.concatenate([keyval[:, head * KV : head * KV + NOPE], rope], axis=1)
        values = keyval[:, head * KV + NOPE : (head + 1) * KV]
        span = slice(head * HEAD, (head + 1) * HEAD)
        query = jnp.concatenate([mine_ref[:, span], other_ref[:, span]], axis=0)
        score = lax.dot_general(
            query, keys, (((1,), (1,)), ((), ())), preferred_element_type=F32
        )
        score = score + bias[...]
        top = jnp.max(score, axis=1, keepdims=True)
        weights = jnp.exp2((score - top) * factor)
        inverse = 1.0 / jnp.sum(weights, axis=1, keepdims=True)
        probs = (weights * inverse).astype(BF16)
        result = jnp.dot(probs, values, preferred_element_type=F32).astype(BF16)
        span = slice(head * VDIM, (head + 1) * VDIM)
        out_ref[:, span] = result[:tokens]
        send_ref[:, span] = result[tokens:]


def attend(where, latent, kv_weight, mine, other):
    tokens = mine.shape[0]
    length = latent.shape[0]
    nodes, chips, rows, columns = kv_weight.shape
    pairs = columns // (2 * KV)
    heads = 2 * pairs * chips
    spec = pltpu.PrefetchScalarGridSpec(
        num_scalar_prefetch=1,
        grid=(chips * pairs,),
        in_specs=[
            pl.BlockSpec((length, LAT + ROPE), lambda i, w: (0, 0)),
            pl.BlockSpec((nodes, 1, rows, 2 * KV), lambda i, w: (0, i // pairs, 0, i % pairs)),
            pl.BlockSpec(
                (tokens, 2 * HEAD), lambda i, w: (0, (2 * (i // pairs) + w[0]) * pairs + i % pairs)
            ),
            pl.BlockSpec((tokens, 2 * HEAD), lambda i, w: (0, i)),
        ],
        out_specs=[
            pl.BlockSpec(
                (tokens, 2 * VDIM), lambda i, w: (0, (2 * (i // pairs) + w[0]) * pairs + i % pairs)
            ),
            pl.BlockSpec((tokens, 2 * VDIM), lambda i, w: (0, i)),
        ],
        scratch_shapes=[pltpu.VMEM((2 * tokens, length), F32)],
    )
    flops = 2 * heads * length * (LAT * KV + 2 * tokens * (HEAD + VDIM))
    return call(
        attention_kernel,
        vmem=48,
        cost=(flops // 4, 2 * (LAT * heads * KV + 4 * tokens * heads * HEAD)),
        grid_spec=spec,
        out_shape=[
            jax.ShapeDtypeStruct((tokens, 2 * heads * VDIM), BF16),
            jax.ShapeDtypeStruct((tokens, heads * VDIM), BF16),
        ],
    )(where, latent, kv_weight, mine, other)


def merge_kernel(where_ref, part_ref, whole_ref, out_ref):
    out_ref[...] = part_ref[...]


def merge(where, part, whole, chips):
    tokens, columns = part.shape
    block = columns // chips
    spec = pltpu.PrefetchScalarGridSpec(
        num_scalar_prefetch=1,
        grid=(chips,),
        in_specs=[
            pl.BlockSpec((tokens, block), lambda i, w: (0, i)),
            pl.BlockSpec(memory_space=pl.ANY),
        ],
        out_specs=pl.BlockSpec((tokens, block), lambda i, w: (0, 2 * i + 1 - w[0])),
    )
    return call(
        merge_kernel,
        cost=(0, 4 * tokens * columns),
        grid_spec=spec,
        out_shape=jax.ShapeDtypeStruct(whole.shape, BF16),
        input_output_aliases={2: 0},
    )(where, part, whole)


def latent_kernel(
    where_ref, hidden_ref, mine_ref, other_ref, gain_ref, cosine_ref, sine_ref, out_ref
):
    core, _, row, col = (where_ref[i] for i in range(4))
    side, blocks, depth = 4, mine_ref.shape[0], mine_ref.shape[1]
    latent = None
    for node in range(blocks):
        by_row = (row + side - node // side) % side
        by_col = (col + side - node % side) % side
        along = by_col * side + by_row
        across = by_row * side + by_col
        start = 2 * depth * node
        lower = hidden_ref[:, start : start + depth]
        upper = hidden_ref[:, start + depth : start + 2 * depth]
        first = core == 0
        for held, block, picked in (
            (mine_ref, jnp.where(first, along, across), jnp.where(first, lower, upper)),
            (other_ref, jnp.where(first, across, along), jnp.where(first, upper, lower)),
        ):
            term = jnp.dot(picked, held[block], preferred_element_type=F32)
            latent = term if latent is None else latent + term
    columns = latent[:, :LAT]
    mean_square = jnp.mean(columns * columns, axis=1, keepdims=True)
    out_ref[:, :LAT] = (columns * lax.rsqrt(mean_square + 1e-06) * gain_ref[...]).astype(BF16)
    keys = latent[:, LAT:]
    half = ROPE // 2
    turned = jnp.concatenate([keys[:, half:], keys[:, :half]], axis=1)
    out_ref[:, LAT:] = (keys * cosine_ref[...] + turned * sine_ref[...]).astype(BF16)


def latents(where, hidden, mine, other, gain, cosine, sine):
    tokens, width = hidden.shape
    spec = pltpu.PrefetchScalarGridSpec(
        num_scalar_prefetch=1,
        grid=(1,),
        in_specs=[
            pl.BlockSpec(array.shape, functools.partial(lambda n, i, w: (0,) * n, array.ndim))
            for array in (hidden, mine, other, gain, cosine, sine)
        ],
        out_specs=pl.BlockSpec((tokens, LAT + ROPE), lambda i, w: (0, 0)),
    )
    return call(
        latent_kernel,
        cost=(2 * tokens * width * (LAT + ROPE), 2 * width * (LAT + ROPE)),
        grid_spec=spec,
        out_shape=jax.ShapeDtypeStruct((tokens, LAT + ROPE), BF16),
    )(where, hidden, mine, other, gain, cosine, sine)


def rotation(position):
    freqs = 10000.0 ** (-2.0 * jnp.arange(ROPE // 2, dtype=F32) / ROPE)
    angles = position.astype(F32)[:, None] * freqs[None, :]
    cosine = jnp.cos(angles)
    sine = jnp.sin(angles)
    return jnp.concatenate([cosine, cosine], axis=1), jnp.concatenate([-sine, sine], axis=1)


def pick_kernel(where_ref, whole_ref, part_ref):
    part_ref[...] = whole_ref[...]


def other_groups(where, queries, groups):
    tokens, columns = queries.shape
    block = columns // groups
    spec = pltpu.PrefetchScalarGridSpec(
        num_scalar_prefetch=1,
        grid=(groups // 2,),
        in_specs=[pl.BlockSpec((tokens, block), lambda i, w: (0, 2 * i + 1 - w[0]))],
        out_specs=pl.BlockSpec((tokens, block), lambda i, w: (0, i)),
    )
    return call(
        pick_kernel,
        cost=(0, 2 * tokens * columns),
        grid_spec=spec,
        out_shape=jax.ShapeDtypeStruct((tokens, columns // 2), BF16),
    )(where, queries)


def swap(array):
    return lax.ppermute(array, "c", [(0, 1), (1, 0)])


def along_x(array, distance):
    size = lax.axis_size("x")
    return lax.ppermute(array, "x", [(i, (i + distance) % size) for i in range(size)])


def turn(array, distance, swapped):
    side = lax.axis_size("z")
    pairs = []
    for row in range(side):
        for col in range(side):
            for core in range(2):
                if (core == 0) != swapped:
                    to = ((row + distance) % side, col)
                else:
                    to = (row, (col + distance) % side)
                pairs.append(((row * side + col) * 2 + core, (to[0] * side + to[1]) * 2 + core))
    return lax.ppermute(array, ("z", "y", "c"), pairs)


def ring(block, swapped):
    return [block] + [turn(block, d, swapped) for d in (1, 3, 2)]


def spread(pieces):
    near, right, left, far = pieces
    return jnp.concatenate([near, right, far, left], axis=0)


def exchange(rows):
    return lax.all_to_all(rows, CHIPS, split_axis=0, concat_axis=0, tiled=True)


def shards(
    hidden,
    latent_weight,
    latent_gain,
    queries,
    kv_weight,
    expert_ids,
    route_weights,
    gate_proj,
    up_proj,
    down_proj,
):
    tokens = hidden.shape[0]
    core = lax.axis_index("c")
    chip = lax.axis_index("x")
    chips = lax.axis_size("x")
    nodes = lax.axis_size("z") * lax.axis_size("y")
    where = jnp.stack([core, chip, lax.axis_index("z"), lax.axis_index("y")]).astype(jnp.int32)

    kv_rows, kv_columns = kv_weight.shape
    kv_all = lax.all_gather(kv_weight, CHIPS, axis=0, tiled=True)
    kv_all = kv_all.reshape(nodes, chips, kv_rows, kv_columns)

    slots = nodes * chips * CAP
    rows, gate = dispatch(expert_ids.T, route_weights.T, hidden, slots)

    depth = latent_weight.shape[0] // 2
    part = lax.dynamic_slice_in_dim(latent_weight, core * depth, depth, axis=0)
    pieces = ring(spread(ring(part[None], False)), True)
    own = (gate_proj, up_proj, down_proj)
    pieces, rows, own, queries = lax.optimization_barrier((pieces, rows, own, queries))
    arrived = exchange(rows)
    mine_weight = spread(pieces)
    other = tuple(swap(array) for array in own)

    position = (2 * chip + core) * tokens + jnp.arange(tokens, dtype=jnp.int32)
    cosine, sine = rotation(position)
    mine = latents(
        where, hidden, mine_weight, swap(mine_weight), latent_gain[None], cosine, sine
    )
    pieces = [mine] + [along_x(mine, d) for d in range(1, chips)]

    results = experts(arrived, own, other)
    pieces, results = lax.optimization_barrier((pieces, results))
    returned = exchange(results)

    line = jnp.concatenate(pieces, axis=0)
    sequence = jnp.concatenate([line, swap(line)], axis=0)

    other_queries = swap(other_groups(where, queries, 2 * chips))

    whole, send = attend(where, sequence, kv_all, queries, other_queries)
    attention = merge(where, swap(send), whole, chips)
    routed = combine(gate, returned)
    return (attention, routed)


def solution(mesh):
    grid = Mesh(mesh.devices.reshape(4, 4, 4, 2), ALL)
    token = P(ALL, None)
    placed = (
        token,
        P(("z", "y"), None),
        P(),
        token,
        P(("z", "y"), ("x", "c")),
        token,
        token,
        P(ALL, None, None),
        P(ALL, None, None),
        P(ALL, None, None),
    )
    return jax.shard_map(
        shards, mesh=grid, in_specs=placed, out_specs=(token, token), check_vma=False
    )
```

```python
import functools
import math

import jax
import jax.numpy as jnp
from jax import lax
from jax.experimental import pallas as pl
from jax.experimental.pallas import tpu as pltpu
from jax.sharding import Mesh
from jax.sharding import PartitionSpec as P

NOPE = 128
ROPE = 64
VDIM = 128
LAT = 512
EXPERTS = 256
TOPK = 8
CAP = 8
HEAD = NOPE + ROPE
KV = NOPE + VDIM
CHIPS = ("z", "y", "x")
ALL = ("z", "y", "x", "c")
BF16 = jnp.bfloat16
F32 = jnp.float32
MIB = 1 << 20


def call(kernel, **options):
    limit = options.pop("vmem", 32)
    flops, moved = options.pop("cost")
    return pl.pallas_call(
        kernel,
        compiler_params=pltpu.CompilerParams(vmem_limit_bytes=limit * MIB),
        cost_estimate=pl.CostEstimate(flops=flops, bytes_accessed=moved, transcendentals=0),
        **options,
    )


def dispatch_kernel(ids_ref, weights_ref, hidden_ref, rows_ref, gate_ref, pick):
    slots, tokens = pick.shape

    @pl.when(pl.program_id(0) == 0)
    def _():
        row = lax.broadcasted_iota(jnp.int32, (slots, tokens), 0)
        number = (row // CAP) * (EXPERTS * CAP // slots)
        named = jnp.zeros((slots, tokens), F32)
        weight = jnp.zeros((slots, tokens), F32)
        for k in range(TOPK):
            here = ids_ref[k : k + 1, :] == number
            named = jnp.where(here, 1.0, named)
            weight = jnp.where(here, weights_ref[k : k + 1, :], weight)
        before = lax.broadcasted_iota(jnp.int32, (tokens, tokens), 0) < lax.broadcasted_iota(
            jnp.int32, (tokens, tokens), 1
        )
        earlier = jnp.dot(
            named.astype(BF16), before.astype(F32).astype(BF16), preferred_element_type=F32
        )
        kept = (named > 0.5) & (earlier.astype(jnp.int32) == row % CAP)
        pick[...] = jnp.where(kept, 1.0, 0.0).astype(BF16)
        gate_ref[...] = jnp.where(kept, weight, 0.0)

    rows_ref[...] = jnp.dot(pick[...], hidden_ref[...], preferred_element_type=F32).astype(BF16)


def dispatch(ids, weights, hidden, slots):
    tokens, width = hidden.shape
    block = 512
    return call(
        dispatch_kernel,
        cost=(2 * slots * tokens * width, 2 * (slots + tokens) * width),
        grid=(width // block,),
        in_specs=[
            pl.BlockSpec((TOPK, tokens), lambda j: (0, 0)),
            pl.BlockSpec((TOPK, tokens), lambda j: (0, 0)),
            pl.BlockSpec((tokens, block), lambda j: (0, j)),
        ],
        out_specs=[
            pl.BlockSpec((slots, block), lambda j: (0, j)),
            pl.BlockSpec((slots, tokens), lambda j: (0, 0)),
        ],
        out_shape=[
            jax.ShapeDtypeStruct((slots, width), BF16),
            jax.ShapeDtypeStruct((slots, tokens), F32),
        ],
        scratch_shapes=[pltpu.VMEM((slots, tokens), BF16)],
    )(ids, weights, hidden)


def combine_kernel(gate_ref, rows_ref, out_ref, terms):
    tokens = out_ref.shape[0]

    @pl.when(pl.program_id(0) == 0)
    def _():
        rest = gate_ref[...].T
        for term in range(3):
            part = rest.astype(BF16)
            terms[term * tokens : (term + 1) * tokens, :] = part
            rest = rest - part.astype(F32)

    total = jnp.dot(terms[...], rows_ref[...], preferred_element_type=F32)
    out_ref[...] = (total[:tokens] + total[tokens : 2 * tokens] + total[2 * tokens :]).astype(BF16)


def combine(gate, rows):
    slots, tokens = gate.shape
    width = rows.shape[1]
    block = 1792
    return call(
        combine_kernel,
        cost=(6 * slots * tokens * width, 2 * (slots + tokens) * width),
        grid=(width // block,),
        in_specs=[
            pl.BlockSpec((slots, tokens), lambda j: (0, 0)),
            pl.BlockSpec((slots, block), lambda j: (0, j)),
        ],
        out_specs=pl.BlockSpec((tokens, block), lambda j: (0, j)),
        out_shape=jax.ShapeDtypeStruct((tokens, width), BF16),
        scratch_shapes=[pltpu.VMEM((3 * tokens, slots), BF16)],
    )(gate, rows)


def expert_kernel(
    rows_ref, gate0, up0, down0, gate1, up1, down1, out_ref, inner, *, steps
):
    step = pl.program_id(0)

    def hidden_block(gate_ref, up_ref):
        rows = rows_ref[...]
        gate = jnp.dot(rows, gate_ref[0], preferred_element_type=F32)
        upper = jnp.dot(rows, up_ref[0], preferred_element_type=F32)
        inner[step] = (gate / (1.0 + jnp.exp(-gate)) * upper).astype(BF16)

    pl.when(step < steps)(lambda: hidden_block(gate0, up0))
    pl.when((step >= steps) & (step < 2 * steps))(lambda: hidden_block(gate1, up1))

    @pl.when(step >= 2 * steps)
    def _():
        wide = inner.shape[2]
        total = None
        for half, down in enumerate((down0, down1)):
            partial = None
            for part in range(steps):
                term = jnp.dot(
                    inner[half * steps + part],
                    down[0, part * wide : (part + 1) * wide, :],
                    preferred_element_type=F32,
                )
                partial = term if partial is None else partial + term
            partial = partial.astype(BF16).astype(F32)
            total = partial if total is None else total + partial
        out_ref[...] = total.astype(BF16)


def experts(rows, own, other):
    count, width = rows.shape
    half = own[0].shape[2]
    wide, block = 256, 1792
    steps = half // wide
    first = 2 * steps

    def column(start):
        return lambda j: (0, 0, jnp.clip(j - start, 0, steps - 1))

    def late(j):
        return (0, 0, jnp.maximum(j - first, 0))

    specs = []
    for start in (0, steps):
        specs += [
            pl.BlockSpec((1, width, wide), column(start)),
            pl.BlockSpec((1, width, wide), column(start)),
            pl.BlockSpec((1, half, block), late),
        ]
    return call(
        functools.partial(expert_kernel, steps=steps),
        vmem=56,
        cost=(12 * count * width * half, 2 * (2 * count * width + 6 * width * half)),
        grid=(first + width // block,),
        in_specs=[pl.BlockSpec((count, width), lambda j: (0, 0))] + specs,
        out_specs=pl.BlockSpec((count, block), lambda j: (0, jnp.maximum(j - first, 0))),
        out_shape=jax.ShapeDtypeStruct((count, width), BF16),
        scratch_shapes=[pltpu.VMEM((first, count, wide), BF16)],
    )(rows, *own, *other)


def attention_kernel(
    where_ref, latent_ref, kv_ref, mine_ref, other_ref, out_ref, send_ref, bias
):
    tokens = mine_ref.shape[0]
    length = latent_ref.shape[0]
    chips = length // (2 * tokens)

    @pl.when(pl.program_id(0) == 0)
    def _():
        core, chip = where_ref[0], where_ref[1]
        row = lax.broadcasted_iota(jnp.int32, (2 * tokens, length), 0)
        col = lax.broadcasted_iota(jnp.int32, (2 * tokens, length), 1)
        row_core = jnp.where(row < tokens, core, 1 - core)
        row_at = (2 * chip + row_core) * tokens + row % tokens
        block = col // tokens
        col_core = jnp.where(block < chips, core, 1 - core)
        col_chip = (chip + chips - block % chips) % chips
        col_at = (2 * col_chip + col_core) * tokens + col % tokens
        bias[...] = jnp.where(col_at <= row_at, 0.0, -1e30)

    compressed = latent_ref[:, :LAT]
    rope = latent_ref[:, LAT:]
    weight = kv_ref[...].reshape(LAT, 2 * KV)
    keyval = jnp.dot(compressed, weight, preferred_element_type=F32).astype(BF16)
    factor = math.log2(math.e) / math.sqrt(HEAD)
    for head in range(2):
        keys = jnp.concatenate([keyval[:, head * KV : head * KV + NOPE], rope], axis=1)
        values = keyval[:, head * KV + NOPE : (head + 1) * KV]
        span = slice(head * HEAD, (head + 1) * HEAD)
        query = jnp.concatenate([mine_ref[:, span], other_ref[:, span]], axis=0)
        score = lax.dot_general(
            query, keys, (((1,), (1,)), ((), ())), preferred_element_type=F32
        )
        score = score + bias[...]
        top = jnp.max(score, axis=1, keepdims=True)
        weights = jnp.exp2((score - top) * factor)
        inverse = 1.0 / jnp.sum(weights, axis=1, keepdims=True)
        probs = (weights * inverse).astype(BF16)
        result = jnp.dot(probs, values, preferred_element_type=F32).astype(BF16)
        span = slice(head * VDIM, (head + 1) * VDIM)
        out_ref[:, span] = result[:tokens]
        send_ref[:, span] = result[tokens:]


def attend(where, latent, kv_weight, mine, other):
    tokens = mine.shape[0]
    length = latent.shape[0]
    nodes, chips, rows, columns = kv_weight.shape
    pairs = columns // (2 * KV)
    heads = 2 * pairs * chips
    spec = pltpu.PrefetchScalarGridSpec(
        num_scalar_prefetch=1,
        grid=(chips * pairs,),
        in_specs=[
            pl.BlockSpec((length, LAT + ROPE), lambda i, w: (0, 0)),
            pl.BlockSpec((nodes, 1, rows, 2 * KV), lambda i, w: (0, i // pairs, 0, i % pairs)),
            pl.BlockSpec(
                (tokens, 2 * HEAD), lambda i, w: (0, (2 * (i // pairs) + w[0]) * pairs + i % pairs)
            ),
            pl.BlockSpec((tokens, 2 * HEAD), lambda i, w: (0, i)),
        ],
        out_specs=[
            pl.BlockSpec(
                (tokens, 2 * VDIM), lambda i, w: (0, (2 * (i // pairs) + w[0]) * pairs + i % pairs)
            ),
            pl.BlockSpec((tokens, 2 * VDIM), lambda i, w: (0, i)),
        ],
        scratch_shapes=[pltpu.VMEM((2 * tokens, length), F32)],
    )
    flops = 2 * heads * length * (LAT * KV + 2 * tokens * (HEAD + VDIM))
    return call(
        attention_kernel,
        vmem=48,
        cost=(flops // 4, 2 * (LAT * heads * KV + 4 * tokens * heads * HEAD)),
        grid_spec=spec,
        out_shape=[
            jax.ShapeDtypeStruct((tokens, 2 * heads * VDIM), BF16),
            jax.ShapeDtypeStruct((tokens, heads * VDIM), BF16),
        ],
    )(where, latent, kv_weight, mine, other)


def merge_kernel(where_ref, part_ref, whole_ref, out_ref):
    out_ref[...] = part_ref[...]


def merge(where, part, whole, chips):
    tokens, columns = part.shape
    block = columns // chips
    spec = pltpu.PrefetchScalarGridSpec(
        num_scalar_prefetch=1,
        grid=(chips,),
        in_specs=[
            pl.BlockSpec((tokens, block), lambda i, w: (0, i)),
            pl.BlockSpec(memory_space=pl.ANY),
        ],
        out_specs=pl.BlockSpec((tokens, block), lambda i, w: (0, 2 * i + 1 - w[0])),
    )
    return call(
        merge_kernel,
        cost=(0, 4 * tokens * columns),
        grid_spec=spec,
        out_shape=jax.ShapeDtypeStruct(whole.shape, BF16),
        input_output_aliases={2: 0},
    )(where, part, whole)


def latent_kernel(
    where_ref, hidden_ref, mine_ref, other_ref, gain_ref, cosine_ref, sine_ref, out_ref
):
    core, _, row, col = (where_ref[i] for i in range(4))
    side, blocks, depth = 4, mine_ref.shape[0], mine_ref.shape[1]
    latent = None
    for node in range(blocks):
        by_row = (row + side - node // side) % side
        by_col = (col + side - node % side) % side
        along = by_col * side + by_row
        across = by_row * side + by_col
        start = 2 * depth * node
        lower = hidden_ref[:, start : start + depth]
        upper = hidden_ref[:, start + depth : start + 2 * depth]
        first = core == 0
        for held, block, picked in (
            (mine_ref, jnp.where(first, along, across), jnp.where(first, lower, upper)),
            (other_ref, jnp.where(first, across, along), jnp.where(first, upper, lower)),
        ):
            term = jnp.dot(picked, held[block], preferred_element_type=F32)
            latent = term if latent is None else latent + term
    columns = latent[:, :LAT]
    mean_square = jnp.mean(columns * columns, axis=1, keepdims=True)
    out_ref[:, :LAT] = (columns * lax.rsqrt(mean_square + 1e-06) * gain_ref[...]).astype(BF16)
    keys = latent[:, LAT:]
    half = ROPE // 2
    turned = jnp.concatenate([keys[:, half:], keys[:, :half]], axis=1)
    out_ref[:, LAT:] = (keys * cosine_ref[...] + turned * sine_ref[...]).astype(BF16)


def latents(where, hidden, mine, other, gain, cosine, sine):
    tokens, width = hidden.shape
    spec = pltpu.PrefetchScalarGridSpec(
        num_scalar_prefetch=1,
        grid=(1,),
        in_specs=[
            pl.BlockSpec(array.shape, functools.partial(lambda n, i, w: (0,) * n, array.ndim))
            for array in (hidden, mine, other, gain, cosine, sine)
        ],
        out_specs=pl.BlockSpec((tokens, LAT + ROPE), lambda i, w: (0, 0)),
    )
    return call(
        latent_kernel,
        cost=(2 * tokens * width * (LAT + ROPE), 2 * width * (LAT + ROPE)),
        grid_spec=spec,
        out_shape=jax.ShapeDtypeStruct((tokens, LAT + ROPE), BF16),
    )(where, hidden, mine, other, gain, cosine, sine)


def rotation(position):
    freqs = 10000.0 ** (-2.0 * jnp.arange(ROPE // 2, dtype=F32) / ROPE)
    angles = position.astype(F32)[:, None] * freqs[None, :]
    cosine = jnp.cos(angles)
    sine = jnp.sin(angles)
    return jnp.concatenate([cosine, cosine], axis=1), jnp.concatenate([-sine, sine], axis=1)


def pick_kernel(where_ref, whole_ref, part_ref):
    part_ref[...] = whole_ref[...]


def other_groups(where, queries, groups):
    tokens, columns = queries.shape
    block = columns // groups
    spec = pltpu.PrefetchScalarGridSpec(
        num_scalar_prefetch=1,
        grid=(groups // 2,),
        in_specs=[pl.BlockSpec((tokens, block), lambda i, w: (0, 2 * i + 1 - w[0]))],
        out_specs=pl.BlockSpec((tokens, block), lambda i, w: (0, i)),
    )
    return call(
        pick_kernel,
        cost=(0, 2 * tokens * columns),
        grid_spec=spec,
        out_shape=jax.ShapeDtypeStruct((tokens, columns // 2), BF16),
    )(where, queries)


def swap(array):
    return lax.ppermute(array, "c", [(0, 1), (1, 0)])


def along_x(array, distance):
    size = lax.axis_size("x")
    return lax.ppermute(array, "x", [(i, (i + distance) % size) for i in range(size)])


def turn(array, distance, swapped):
    side = lax.axis_size("z")
    pairs = []
    for row in range(side):
        for col in range(side):
            for core in range(2):
                if (core == 0) != swapped:
                    to = ((row + distance) % side, col)
                else:
                    to = (row, (col + distance) % side)
                pairs.append(((row * side + col) * 2 + core, (to[0] * side + to[1]) * 2 + core))
    return lax.ppermute(array, ("z", "y", "c"), pairs)


def ring(block, swapped):
    return [block] + [turn(block, d, swapped) for d in (1, 3, 2)]


def spread(pieces):
    near, right, left, far = pieces
    return jnp.concatenate([near, right, far, left], axis=0)


def exchange(rows):
    return lax.all_to_all(rows, CHIPS, split_axis=0, concat_axis=0, tiled=True)


def shards(
    hidden,
    latent_weight,
    latent_gain,
    queries,
    kv_weight,
    expert_ids,
    route_weights,
    gate_proj,
    up_proj,
    down_proj,
):
    tokens = hidden.shape[0]
    core = lax.axis_index("c")
    chip = lax.axis_index("x")
    chips = lax.axis_size("x")
    nodes = lax.axis_size("z") * lax.axis_size("y")
    where = jnp.stack([core, chip, lax.axis_index("z"), lax.axis_index("y")]).astype(jnp.int32)

    kv_rows, kv_columns = kv_weight.shape
    kv_all = lax.all_gather(kv_weight, CHIPS, axis=0, tiled=True)
    kv_all = kv_all.reshape(nodes, chips, kv_rows, kv_columns)

    slots = nodes * chips * CAP
    rows, gate = dispatch(expert_ids.T, route_weights.T, hidden, slots)

    depth = latent_weight.shape[0] // 2
    part = lax.dynamic_slice_in_dim(latent_weight, core * depth, depth, axis=0)
    pieces = ring(spread(ring(part[None], False)), True)
    own = (gate_proj, up_proj, down_proj)
    pieces, rows, own, queries = lax.optimization_barrier((pieces, rows, own, queries))
    arrived = exchange(rows)
    mine_weight = spread(pieces)
    other = tuple(swap(array) for array in own)
    other_queries = swap(other_groups(where, queries, 2 * chips))

    position = (2 * chip + core) * tokens + jnp.arange(tokens, dtype=jnp.int32)
    cosine, sine = rotation(position)
    mine = latents(
        where, hidden, mine_weight, swap(mine_weight), latent_gain[None], cosine, sine
    )
    pieces = [mine] + [along_x(mine, d) for d in range(1, chips)]

    results = experts(arrived, own, other)
    pieces, results = lax.optimization_barrier((pieces, results))
    line = jnp.concatenate(pieces, axis=0)
    sequence = jnp.concatenate([line, swap(line)], axis=0)
    sequence, results = lax.optimization_barrier((sequence, results))
    returned = exchange(results)

    whole, send = attend(where, sequence, kv_all, queries, other_queries)
    attention = merge(where, swap(send), whole, chips)
    attention, returned = lax.optimization_barrier((attention, returned))
    routed = combine(gate, returned)
    return (attention, routed)


def solution(mesh):
    grid = Mesh(mesh.devices.reshape(4, 4, 4, 2), ALL)
    token = P(ALL, None)
    placed = (
        token,
        P(("z", "y"), None),
        P(),
        token,
        P(("z", "y"), ("x", "c")),
        token,
        token,
        P(ALL, None, None),
        P(ALL, None, None),
        P(ALL, None, None),
    )
    return jax.shard_map(
        shards, mesh=grid, in_specs=placed, out_specs=(token, token), check_vma=False
    )
```

```python
import functools
import math

import jax
import jax.numpy as jnp
from jax import lax
from jax.experimental import pallas as pl
from jax.experimental.pallas import tpu as pltpu
from jax.sharding import Mesh
from jax.sharding import PartitionSpec as P

NOPE = 128
ROPE = 64
VDIM = 128
LAT = 512
EXPERTS = 256
TOPK = 8
CAP = 8
HEAD = NOPE + ROPE
KV = NOPE + VDIM
CHIPS = ("z", "y", "x")
ALL = ("z", "y", "x", "c")
BF16 = jnp.bfloat16
F32 = jnp.float32
MIB = 1 << 20


def call(kernel, **options):
    limit = options.pop("vmem", 32)
    flops, moved = options.pop("cost")
    return pl.pallas_call(
        kernel,
        compiler_params=pltpu.CompilerParams(vmem_limit_bytes=limit * MIB),
        cost_estimate=pl.CostEstimate(flops=flops, bytes_accessed=moved, transcendentals=0),
        **options,
    )


def dispatch_kernel(ids_ref, weights_ref, hidden_ref, rows_ref, gate_ref, pick):
    slots, tokens = pick.shape

    @pl.when(pl.program_id(0) == 0)
    def _():
        row = lax.broadcasted_iota(jnp.int32, (slots, tokens), 0)
        number = (row // CAP) * (EXPERTS * CAP // slots)
        named = jnp.zeros((slots, tokens), F32)
        weight = jnp.zeros((slots, tokens), F32)
        for k in range(TOPK):
            here = ids_ref[k : k + 1, :] == number
            named = jnp.where(here, 1.0, named)
            weight = jnp.where(here, weights_ref[k : k + 1, :], weight)
        before = lax.broadcasted_iota(jnp.int32, (tokens, tokens), 0) < lax.broadcasted_iota(
            jnp.int32, (tokens, tokens), 1
        )
        earlier = jnp.dot(
            named.astype(BF16), before.astype(F32).astype(BF16), preferred_element_type=F32
        )
        kept = (named > 0.5) & (earlier.astype(jnp.int32) == row % CAP)
        pick[...] = jnp.where(kept, 1.0, 0.0).astype(BF16)
        gate_ref[...] = jnp.where(kept, weight, 0.0)

    rows_ref[...] = jnp.dot(pick[...], hidden_ref[...], preferred_element_type=F32).astype(BF16)


def dispatch(ids, weights, hidden, slots):
    tokens, width = hidden.shape
    block = 512
    return call(
        dispatch_kernel,
        cost=(2 * slots * tokens * width, 2 * (slots + tokens) * width),
        grid=(width // block,),
        in_specs=[
            pl.BlockSpec((TOPK, tokens), lambda j: (0, 0)),
            pl.BlockSpec((TOPK, tokens), lambda j: (0, 0)),
            pl.BlockSpec((tokens, block), lambda j: (0, j)),
        ],
        out_specs=[
            pl.BlockSpec((slots, block), lambda j: (0, j)),
            pl.BlockSpec((slots, tokens), lambda j: (0, 0)),
        ],
        out_shape=[
            jax.ShapeDtypeStruct((slots, width), BF16),
            jax.ShapeDtypeStruct((slots, tokens), F32),
        ],
        scratch_shapes=[pltpu.VMEM((slots, tokens), BF16)],
    )(ids, weights, hidden)


def combine_kernel(gate_ref, rows_ref, out_ref, terms):
    tokens = out_ref.shape[0]

    @pl.when(pl.program_id(0) == 0)
    def _():
        rest = gate_ref[...].T
        for term in range(3):
            part = rest.astype(BF16)
            terms[term * tokens : (term + 1) * tokens, :] = part
            rest = rest - part.astype(F32)

    total = jnp.dot(terms[...], rows_ref[...], preferred_element_type=F32)
    out_ref[...] = (total[:tokens] + total[tokens : 2 * tokens] + total[2 * tokens :]).astype(BF16)


def combine(gate, rows):
    slots, tokens = gate.shape
    width = rows.shape[1]
    block = 1792
    return call(
        combine_kernel,
        cost=(6 * slots * tokens * width, 2 * (slots + tokens) * width),
        grid=(width // block,),
        in_specs=[
            pl.BlockSpec((slots, tokens), lambda j: (0, 0)),
            pl.BlockSpec((slots, block), lambda j: (0, j)),
        ],
        out_specs=pl.BlockSpec((tokens, block), lambda j: (0, j)),
        out_shape=jax.ShapeDtypeStruct((tokens, width), BF16),
        scratch_shapes=[pltpu.VMEM((3 * tokens, slots), BF16)],
    )(gate, rows)


def expert_kernel(
    rows_ref, gate0, up0, down0, gate1, up1, down1, out_ref, inner, *, steps
):
    step = pl.program_id(0)

    def hidden_block(gate_ref, up_ref):
        rows = rows_ref[...]
        gate = jnp.dot(rows, gate_ref[0], preferred_element_type=F32)
        upper = jnp.dot(rows, up_ref[0], preferred_element_type=F32)
        inner[step] = (gate / (1.0 + jnp.exp(-gate)) * upper).astype(BF16)

    pl.when(step < steps)(lambda: hidden_block(gate0, up0))
    pl.when((step >= steps) & (step < 2 * steps))(lambda: hidden_block(gate1, up1))

    @pl.when(step >= 2 * steps)
    def _():
        wide = inner.shape[2]
        total = None
        for half, down in enumerate((down0, down1)):
            partial = None
            for part in range(steps):
                term = jnp.dot(
                    inner[half * steps + part],
                    down[0, part * wide : (part + 1) * wide, :],
                    preferred_element_type=F32,
                )
                partial = term if partial is None else partial + term
            partial = partial.astype(BF16).astype(F32)
            total = partial if total is None else total + partial
        out_ref[...] = total.astype(BF16)


def experts(rows, own, other):
    count, width = rows.shape
    half = own[0].shape[2]
    wide, block = 256, 1792
    steps = half // wide
    first = 2 * steps

    def column(start):
        return lambda j: (0, 0, jnp.clip(j - start, 0, steps - 1))

    def late(j):
        return (0, 0, jnp.maximum(j - first, 0))

    specs = []
    for start in (0, steps):
        specs += [
            pl.BlockSpec((1, width, wide), column(start)),
            pl.BlockSpec((1, width, wide), column(start)),
            pl.BlockSpec((1, half, block), late),
        ]
    return call(
        functools.partial(expert_kernel, steps=steps),
        vmem=56,
        cost=(12 * count * width * half, 2 * (2 * count * width + 6 * width * half)),
        grid=(first + width // block,),
        in_specs=[pl.BlockSpec((count, width), lambda j: (0, 0))] + specs,
        out_specs=pl.BlockSpec((count, block), lambda j: (0, jnp.maximum(j - first, 0))),
        out_shape=jax.ShapeDtypeStruct((count, width), BF16),
        scratch_shapes=[pltpu.VMEM((first, count, wide), BF16)],
    )(rows, *own, *other)


def attention_kernel(
    where_ref, latent_ref, kv_ref, mine_ref, other_ref, out_ref, send_ref, bias
):
    tokens = mine_ref.shape[0]
    length = latent_ref.shape[0]
    chips = length // (2 * tokens)

    @pl.when(pl.program_id(0) == 0)
    def _():
        core, chip = where_ref[0], where_ref[1]
        row = lax.broadcasted_iota(jnp.int32, (length, 2 * tokens), 1)
        col = lax.broadcasted_iota(jnp.int32, (length, 2 * tokens), 0)
        row_core = jnp.where(row < tokens, core, 1 - core)
        row_at = (2 * chip + row_core) * tokens + row % tokens
        block = col // tokens
        col_core = jnp.where(block < chips, core, 1 - core)
        col_chip = (chip + chips - block % chips) % chips
        col_at = (2 * col_chip + col_core) * tokens + col % tokens
        bias[...] = jnp.where(col_at <= row_at, 0.0, -1e30)

    compressed = latent_ref[:, :LAT]
    rope = latent_ref[:, LAT:]
    group = kv_ref.shape[3] // KV
    weight = kv_ref[...].reshape(LAT, group * KV)
    keyval = jnp.dot(compressed, weight, preferred_element_type=F32).astype(BF16)
    factor = math.log2(math.e) / math.sqrt(HEAD)
    for head in range(group):
        keys = jnp.concatenate([keyval[:, head * KV : head * KV + NOPE], rope], axis=1)
        values = keyval[:, head * KV + NOPE : (head + 1) * KV]
        span = slice(head * HEAD, (head + 1) * HEAD)
        query = jnp.concatenate([mine_ref[:, span], other_ref[:, span]], axis=0)
        score = lax.dot_general(
            keys, query, (((1,), (1,)), ((), ())), preferred_element_type=F32
        )
        score = score + bias[...]
        top = jnp.max(score, axis=0, keepdims=True)
        weights = jnp.exp2((score - top) * factor)
        inverse = 1.0 / jnp.sum(weights, axis=0, keepdims=True)
        probs = (weights * inverse).astype(BF16)
        result = lax.dot_general(
            probs, values, (((0,), (0,)), ((), ())), preferred_element_type=F32
        ).astype(BF16)
        span = slice(head * VDIM, (head + 1) * VDIM)
        out_ref[:, span] = result[:tokens]
        send_ref[:, span] = result[tokens:]


def attend(where, latent, kv_weight, mine, other):
    tokens = mine.shape[0]
    length = latent.shape[0]
    nodes, chips, rows, columns = kv_weight.shape
    group = columns // KV
    heads = group * chips
    spec = pltpu.PrefetchScalarGridSpec(
        num_scalar_prefetch=1,
        grid=(chips,),
        in_specs=[
            pl.BlockSpec((length, LAT + ROPE), lambda i, w: (0, 0)),
            pl.BlockSpec((nodes, 1, rows, group * KV), lambda i, w: (0, i, 0, 0)),
            pl.BlockSpec(
                (tokens, group * HEAD), lambda i, w: (0, 2 * i + w[0])
            ),
            pl.BlockSpec((tokens, group * HEAD), lambda i, w: (0, i)),
        ],
        out_specs=[
            pl.BlockSpec(
                (tokens, group * VDIM), lambda i, w: (0, 2 * i + w[0])
            ),
            pl.BlockSpec((tokens, group * VDIM), lambda i, w: (0, i)),
        ],
        scratch_shapes=[pltpu.VMEM((length, 2 * tokens), F32)],
    )
    flops = 2 * heads * length * (LAT * KV + 2 * tokens * (HEAD + VDIM))
    return call(
        attention_kernel,
        vmem=48,
        cost=(flops // 4, 2 * (LAT * heads * KV + 4 * tokens * heads * HEAD)),
        grid_spec=spec,
        out_shape=[
            jax.ShapeDtypeStruct((tokens, 2 * heads * VDIM), BF16),
            jax.ShapeDtypeStruct((tokens, heads * VDIM), BF16),
        ],
    )(where, latent, kv_weight, mine, other)


def merge_kernel(where_ref, part_ref, whole_ref, out_ref):
    out_ref[...] = part_ref[...]


def merge(where, part, whole, chips):
    tokens, columns = part.shape
    block = columns // chips
    spec = pltpu.PrefetchScalarGridSpec(
        num_scalar_prefetch=1,
        grid=(chips,),
        in_specs=[
            pl.BlockSpec((tokens, block), lambda i, w: (0, i)),
            pl.BlockSpec(memory_space=pl.ANY),
        ],
        out_specs=pl.BlockSpec((tokens, block), lambda i, w: (0, 2 * i + 1 - w[0])),
    )
    return call(
        merge_kernel,
        cost=(0, 4 * tokens * columns),
        grid_spec=spec,
        out_shape=jax.ShapeDtypeStruct(whole.shape, BF16),
        input_output_aliases={2: 0},
    )(where, part, whole)


def latent_kernel(
    where_ref, hidden_ref, mine_ref, other_ref, gain_ref, cosine_ref, sine_ref, out_ref
):
    core, _, row, col = (where_ref[i] for i in range(4))
    side, blocks, depth = 4, mine_ref.shape[0], mine_ref.shape[1]
    latent = None
    for node in range(blocks):
        by_row = (row + side - node // side) % side
        by_col = (col + side - node % side) % side
        along = by_col * side + by_row
        across = by_row * side + by_col
        start = 2 * depth * node
        lower = hidden_ref[:, start : start + depth]
        upper = hidden_ref[:, start + depth : start + 2 * depth]
        first = core == 0
        for held, block, picked in (
            (mine_ref, jnp.where(first, along, across), jnp.where(first, lower, upper)),
            (other_ref, jnp.where(first, across, along), jnp.where(first, upper, lower)),
        ):
            term = jnp.dot(picked, held[block], preferred_element_type=F32)
            latent = term if latent is None else latent + term
    columns = latent[:, :LAT]
    mean_square = jnp.mean(columns * columns, axis=1, keepdims=True)
    out_ref[:, :LAT] = (columns * lax.rsqrt(mean_square + 1e-06) * gain_ref[...]).astype(BF16)
    keys = latent[:, LAT:]
    half = ROPE // 2
    turned = jnp.concatenate([keys[:, half:], keys[:, :half]], axis=1)
    out_ref[:, LAT:] = (keys * cosine_ref[...] + turned * sine_ref[...]).astype(BF16)


def latents(where, hidden, mine, other, gain, cosine, sine):
    tokens, width = hidden.shape
    spec = pltpu.PrefetchScalarGridSpec(
        num_scalar_prefetch=1,
        grid=(1,),
        in_specs=[
            pl.BlockSpec(array.shape, functools.partial(lambda n, i, w: (0,) * n, array.ndim))
            for array in (hidden, mine, other, gain, cosine, sine)
        ],
        out_specs=pl.BlockSpec((tokens, LAT + ROPE), lambda i, w: (0, 0)),
    )
    return call(
        latent_kernel,
        cost=(2 * tokens * width * (LAT + ROPE), 2 * width * (LAT + ROPE)),
        grid_spec=spec,
        out_shape=jax.ShapeDtypeStruct((tokens, LAT + ROPE), BF16),
    )(where, hidden, mine, other, gain, cosine, sine)


def rotation(position):
    freqs = 10000.0 ** (-2.0 * jnp.arange(ROPE // 2, dtype=F32) / ROPE)
    angles = position.astype(F32)[:, None] * freqs[None, :]
    cosine = jnp.cos(angles)
    sine = jnp.sin(angles)
    return jnp.concatenate([cosine, cosine], axis=1), jnp.concatenate([-sine, sine], axis=1)


def pick_kernel(where_ref, whole_ref, part_ref):
    part_ref[...] = whole_ref[...]


def other_groups(where, queries, groups):
    tokens, columns = queries.shape
    block = columns // groups
    spec = pltpu.PrefetchScalarGridSpec(
        num_scalar_prefetch=1,
        grid=(groups // 2,),
        in_specs=[pl.BlockSpec((tokens, block), lambda i, w: (0, 2 * i + 1 - w[0]))],
        out_specs=pl.BlockSpec((tokens, block), lambda i, w: (0, i)),
    )
    return call(
        pick_kernel,
        cost=(0, 2 * tokens * columns),
        grid_spec=spec,
        out_shape=jax.ShapeDtypeStruct((tokens, columns // 2), BF16),
    )(where, queries)


def swap(array):
    return lax.ppermute(array, "c", [(0, 1), (1, 0)])


def along_x(array, distance):
    size = lax.axis_size("x")
    return lax.ppermute(array, "x", [(i, (i + distance) % size) for i in range(size)])


def turn(array, distance, swapped):
    side = lax.axis_size("z")
    pairs = []
    for row in range(side):
        for col in range(side):
            for core in range(2):
                if (core == 0) != swapped:
                    to = ((row + distance) % side, col)
                else:
                    to = (row, (col + distance) % side)
                pairs.append(((row * side + col) * 2 + core, (to[0] * side + to[1]) * 2 + core))
    return lax.ppermute(array, ("z", "y", "c"), pairs)


def ring(block, swapped):
    return [block] + [turn(block, d, swapped) for d in (1, 3, 2)]


def spread(pieces):
    near, right, left, far = pieces
    return jnp.concatenate([near, right, far, left], axis=0)


def exchange(rows):
    return lax.all_to_all(rows, CHIPS, split_axis=0, concat_axis=0, tiled=True)


def shards(
    hidden,
    latent_weight,
    latent_gain,
    queries,
    kv_weight,
    expert_ids,
    route_weights,
    gate_proj,
    up_proj,
    down_proj,
):
    tokens = hidden.shape[0]
    core = lax.axis_index("c")
    chip = lax.axis_index("x")
    chips = lax.axis_size("x")
    nodes = lax.axis_size("z") * lax.axis_size("y")
    where = jnp.stack([core, chip, lax.axis_index("z"), lax.axis_index("y")]).astype(jnp.int32)

    kv_rows, kv_columns = kv_weight.shape
    kv_all = lax.all_gather(kv_weight, CHIPS, axis=0, tiled=True)
    kv_all = kv_all.reshape(nodes, chips, kv_rows, kv_columns)

    slots = nodes * chips * CAP
    rows, gate = dispatch(expert_ids.T, route_weights.T, hidden, slots)

    depth = latent_weight.shape[0] // 2
    part = lax.dynamic_slice_in_dim(latent_weight, core * depth, depth, axis=0)
    pieces = ring(spread(ring(part[None], False)), True)
    own = (gate_proj, up_proj, down_proj)
    pieces, rows, own, queries = lax.optimization_barrier((pieces, rows, own, queries))
    arrived = exchange(rows)
    mine_weight = spread(pieces)
    other = tuple(swap(array) for array in own)
    other_queries = swap(other_groups(where, queries, 2 * chips))

    position = (2 * chip + core) * tokens + jnp.arange(tokens, dtype=jnp.int32)
    cosine, sine = rotation(position)
    mine = latents(
        where, hidden, mine_weight, swap(mine_weight), latent_gain[None], cosine, sine
    )
    pieces = [mine] + [along_x(mine, d) for d in range(1, chips)]

    results = experts(arrived, own, other)
    pieces, results = lax.optimization_barrier((pieces, results))
    line = jnp.concatenate(pieces, axis=0)
    sequence = jnp.concatenate([line, swap(line)], axis=0)
    returned = exchange(results)

    whole, send = attend(where, sequence, kv_all, queries, other_queries)
    attention = merge(where, swap(send), whole, chips)
    attention, returned = lax.optimization_barrier((attention, returned))
    routed = combine(gate, returned)
    return (attention, routed)


def solution(mesh):
    grid = Mesh(mesh.devices.reshape(4, 4, 4, 2), ALL)
    token = P(ALL, None)
    placed = (
        token,
        P(("z", "y"), None),
        P(),
        token,
        P(("z", "y"), ("x", "c")),
        token,
        token,
        P(ALL, None, None),
        P(ALL, None, None),
        P(ALL, None, None),
    )
    return jax.shard_map(
        shards, mesh=grid, in_specs=placed, out_specs=(token, token), check_vma=False
    )
```

```python
import functools
import math

import jax
import jax.numpy as jnp
from jax import lax
from jax.experimental import pallas as pl
from jax.experimental.pallas import tpu as pltpu
from jax.sharding import Mesh
from jax.sharding import PartitionSpec as P

NOPE = 128
ROPE = 64
VDIM = 128
LAT = 512
EXPERTS = 256
TOPK = 8
CAP = 8
HEAD = NOPE + ROPE
KV = NOPE + VDIM
CHIPS = ("z", "y", "x")
ALL = ("z", "y", "x", "c")
BF16 = jnp.bfloat16
F32 = jnp.float32
MIB = 1 << 20


def call(kernel, **options):
    limit = options.pop("vmem", 32)
    flops, moved = options.pop("cost")
    return pl.pallas_call(
        kernel,
        compiler_params=pltpu.CompilerParams(vmem_limit_bytes=limit * MIB),
        cost_estimate=pl.CostEstimate(flops=flops, bytes_accessed=moved, transcendentals=0),
        **options,
    )


def dispatch_kernel(ids_ref, weights_ref, hidden_ref, rows_ref, gate_ref, pick):
    slots, tokens = pick.shape

    @pl.when(pl.program_id(0) == 0)
    def _():
        row = lax.broadcasted_iota(jnp.int32, (slots, tokens), 0)
        number = (row // CAP) * (EXPERTS * CAP // slots)
        named = jnp.zeros((slots, tokens), F32)
        weight = jnp.zeros((slots, tokens), F32)
        for k in range(TOPK):
            here = ids_ref[k : k + 1, :] == number
            named = jnp.where(here, 1.0, named)
            weight = jnp.where(here, weights_ref[k : k + 1, :], weight)
        before = lax.broadcasted_iota(jnp.int32, (tokens, tokens), 0) < lax.broadcasted_iota(
            jnp.int32, (tokens, tokens), 1
        )
        earlier = jnp.dot(
            named.astype(BF16), before.astype(F32).astype(BF16), preferred_element_type=F32
        )
        kept = (named > 0.5) & (earlier.astype(jnp.int32) == row % CAP)
        pick[...] = jnp.where(kept, 1.0, 0.0).astype(BF16)
        gate_ref[...] = jnp.where(kept, weight, 0.0)

    rows_ref[...] = jnp.dot(pick[...], hidden_ref[...], preferred_element_type=F32).astype(BF16)


def dispatch(ids, weights, hidden, slots):
    tokens, width = hidden.shape
    block = 512
    return call(
        dispatch_kernel,
        cost=(2 * slots * tokens * width, 2 * (slots + tokens) * width),
        grid=(width // block,),
        in_specs=[
            pl.BlockSpec((TOPK, tokens), lambda j: (0, 0)),
            pl.BlockSpec((TOPK, tokens), lambda j: (0, 0)),
            pl.BlockSpec((tokens, block), lambda j: (0, j)),
        ],
        out_specs=[
            pl.BlockSpec((slots, block), lambda j: (0, j)),
            pl.BlockSpec((slots, tokens), lambda j: (0, 0)),
        ],
        out_shape=[
            jax.ShapeDtypeStruct((slots, width), BF16),
            jax.ShapeDtypeStruct((slots, tokens), F32),
        ],
        scratch_shapes=[pltpu.VMEM((slots, tokens), BF16)],
    )(ids, weights, hidden)


def combine_kernel(gate_ref, rows_ref, out_ref, terms):
    tokens = out_ref.shape[0]

    @pl.when(pl.program_id(0) == 0)
    def _():
        rest = gate_ref[...].T
        for term in range(3):
            part = rest.astype(BF16)
            terms[term * tokens : (term + 1) * tokens, :] = part
            rest = rest - part.astype(F32)

    total = jnp.dot(terms[...], rows_ref[...], preferred_element_type=F32)
    out_ref[...] = (total[:tokens] + total[tokens : 2 * tokens] + total[2 * tokens :]).astype(BF16)


def combine(gate, rows):
    slots, tokens = gate.shape
    width = rows.shape[1]
    block = 1792
    return call(
        combine_kernel,
        cost=(6 * slots * tokens * width, 2 * (slots + tokens) * width),
        grid=(width // block,),
        in_specs=[
            pl.BlockSpec((slots, tokens), lambda j: (0, 0)),
            pl.BlockSpec((slots, block), lambda j: (0, j)),
        ],
        out_specs=pl.BlockSpec((tokens, block), lambda j: (0, j)),
        out_shape=jax.ShapeDtypeStruct((tokens, width), BF16),
        scratch_shapes=[pltpu.VMEM((3 * tokens, slots), BF16)],
    )(gate, rows)


def expert_kernel(
    rows_ref, gate0, up0, down0, gate1, up1, down1, out_ref, inner, *, steps
):
    step = pl.program_id(0)

    def hidden_block(gate_ref, up_ref):
        rows = rows_ref[...]
        gate = jnp.dot(rows, gate_ref[0], preferred_element_type=F32)
        upper = jnp.dot(rows, up_ref[0], preferred_element_type=F32)
        inner[step] = (gate / (1.0 + jnp.exp(-gate)) * upper).astype(BF16)

    pl.when(step < steps)(lambda: hidden_block(gate0, up0))
    pl.when((step >= steps) & (step < 2 * steps))(lambda: hidden_block(gate1, up1))

    @pl.when(step >= 2 * steps)
    def _():
        wide = inner.shape[2]
        total = None
        for half, down in enumerate((down0, down1)):
            partial = None
            for part in range(steps):
                term = jnp.dot(
                    inner[half * steps + part],
                    down[0, part * wide : (part + 1) * wide, :],
                    preferred_element_type=F32,
                )
                partial = term if partial is None else partial + term
            partial = partial.astype(BF16).astype(F32)
            total = partial if total is None else total + partial
        out_ref[...] = total.astype(BF16)


def experts(rows, own, other):
    count, width = rows.shape
    half = own[0].shape[2]
    wide, block = 256, 1792
    steps = half // wide
    first = 2 * steps

    def column(start):
        return lambda j: (0, 0, jnp.clip(j - start, 0, steps - 1))

    def late(j):
        return (0, 0, jnp.maximum(j - first, 0))

    specs = []
    for start in (0, steps):
        specs += [
            pl.BlockSpec((1, width, wide), column(start)),
            pl.BlockSpec((1, width, wide), column(start)),
            pl.BlockSpec((1, half, block), late),
        ]
    return call(
        functools.partial(expert_kernel, steps=steps),
        vmem=56,
        cost=(12 * count * width * half, 2 * (2 * count * width + 6 * width * half)),
        grid=(first + width // block,),
        in_specs=[pl.BlockSpec((count, width), lambda j: (0, 0))] + specs,
        out_specs=pl.BlockSpec((count, block), lambda j: (0, jnp.maximum(j - first, 0))),
        out_shape=jax.ShapeDtypeStruct((count, width), BF16),
        scratch_shapes=[pltpu.VMEM((first, count, wide), BF16)],
    )(rows, *own, *other)


def attention_kernel(
    where_ref, latent_ref, kv_ref, mine_ref, other_ref, out_ref, send_ref, bias
):
    tokens = mine_ref.shape[0]
    length = latent_ref.shape[0]
    chips = length // (2 * tokens)

    @pl.when(pl.program_id(0) == 0)
    def _():
        core, chip = where_ref[0], where_ref[1]
        row = lax.broadcasted_iota(jnp.int32, (length, 2 * tokens), 1)
        col = lax.broadcasted_iota(jnp.int32, (length, 2 * tokens), 0)
        row_core = jnp.where(row < tokens, core, 1 - core)
        row_at = (2 * chip + row_core) * tokens + row % tokens
        block = col // tokens
        col_core = jnp.where(block < chips, core, 1 - core)
        col_chip = (chip + chips - block % chips) % chips
        col_at = (2 * col_chip + col_core) * tokens + col % tokens
        bias[...] = jnp.where(col_at <= row_at, 0.0, -1e30)

    compressed = latent_ref[:, :LAT]
    rope = latent_ref[:, LAT:]
    group = kv_ref.shape[3] // KV
    weight = kv_ref[...].reshape(LAT, group * KV)
    keyval = jnp.dot(compressed, weight, preferred_element_type=F32).astype(BF16)
    factor = math.log2(math.e) / math.sqrt(HEAD)
    for head in range(group):
        keys = jnp.concatenate([keyval[:, head * KV : head * KV + NOPE], rope], axis=1)
        values = keyval[:, head * KV + NOPE : (head + 1) * KV]
        span = slice(head * HEAD, (head + 1) * HEAD)
        query = jnp.concatenate([mine_ref[:, span], other_ref[:, span]], axis=0)
        score = lax.dot_general(
            keys, query, (((1,), (1,)), ((), ())), preferred_element_type=F32
        )
        score = score + bias[...]
        top = jnp.max(score, axis=0, keepdims=True)
        weights = jnp.exp2((score - top) * factor)
        inverse = 1.0 / jnp.sum(weights, axis=0, keepdims=True)
        probs = (weights * inverse).astype(BF16)
        result = lax.dot_general(
            probs, values, (((0,), (0,)), ((), ())), preferred_element_type=F32
        ).astype(BF16)
        span = slice(head * VDIM, (head + 1) * VDIM)
        out_ref[:, span] = result[:tokens]
        send_ref[:, span] = result[tokens:]


def attend(where, latent, kv_weight, mine, other):
    tokens = mine.shape[0]
    length = latent.shape[0]
    nodes, chips, rows, columns = kv_weight.shape
    group = columns // KV
    heads = group * chips
    spec = pltpu.PrefetchScalarGridSpec(
        num_scalar_prefetch=1,
        grid=(chips,),
        in_specs=[
            pl.BlockSpec((length, LAT + ROPE), lambda i, w: (0, 0)),
            pl.BlockSpec((nodes, 1, rows, group * KV), lambda i, w: (0, i, 0, 0)),
            pl.BlockSpec(
                (tokens, group * HEAD), lambda i, w: (0, 2 * i + w[0])
            ),
            pl.BlockSpec((tokens, group * HEAD), lambda i, w: (0, i)),
        ],
        out_specs=[
            pl.BlockSpec(
                (tokens, group * VDIM), lambda i, w: (0, 2 * i + w[0])
            ),
            pl.BlockSpec((tokens, group * VDIM), lambda i, w: (0, i)),
        ],
        scratch_shapes=[pltpu.VMEM((length, 2 * tokens), F32)],
    )
    flops = 2 * heads * length * (LAT * KV + 2 * tokens * (HEAD + VDIM))
    return call(
        attention_kernel,
        vmem=48,
        cost=(flops // 4, 2 * (LAT * heads * KV + 4 * tokens * heads * HEAD)),
        grid_spec=spec,
        out_shape=[
            jax.ShapeDtypeStruct((tokens, 2 * heads * VDIM), BF16),
            jax.ShapeDtypeStruct((tokens, heads * VDIM), BF16),
        ],
    )(where, latent, kv_weight, mine, other)


def merge_kernel(where_ref, part_ref, whole_ref, out_ref):
    out_ref[...] = part_ref[...]


def merge(where, part, whole, chips):
    tokens, columns = part.shape
    block = columns // chips
    spec = pltpu.PrefetchScalarGridSpec(
        num_scalar_prefetch=1,
        grid=(chips,),
        in_specs=[
            pl.BlockSpec((tokens, block), lambda i, w: (0, i)),
            pl.BlockSpec(memory_space=pl.ANY),
        ],
        out_specs=pl.BlockSpec((tokens, block), lambda i, w: (0, 2 * i + 1 - w[0])),
    )
    return call(
        merge_kernel,
        cost=(0, 4 * tokens * columns),
        grid_spec=spec,
        out_shape=jax.ShapeDtypeStruct(whole.shape, BF16),
        input_output_aliases={2: 0},
    )(where, part, whole)


def latent_kernel(
    where_ref, hidden_ref, mine_ref, other_ref, gain_ref, cosine_ref, sine_ref, out_ref
):
    core, _, row, col = (where_ref[i] for i in range(4))
    side, blocks, depth = 4, mine_ref.shape[0], mine_ref.shape[1]
    latent = None
    for node in range(blocks):
        by_row = (row + side - node // side) % side
        by_col = (col + side - node % side) % side
        along = by_col * side + by_row
        across = by_row * side + by_col
        start = 2 * depth * node
        lower = hidden_ref[:, start : start + depth]
        upper = hidden_ref[:, start + depth : start + 2 * depth]
        first = core == 0
        for held, block, picked in (
            (mine_ref, jnp.where(first, along, across), jnp.where(first, lower, upper)),
            (other_ref, jnp.where(first, across, along), jnp.where(first, upper, lower)),
        ):
            term = jnp.dot(picked, held[block], preferred_element_type=F32)
            latent = term if latent is None else latent + term
    columns = latent[:, :LAT]
    mean_square = jnp.mean(columns * columns, axis=1, keepdims=True)
    out_ref[:, :LAT] = (columns * lax.rsqrt(mean_square + 1e-06) * gain_ref[...]).astype(BF16)
    keys = latent[:, LAT:]
    half = ROPE // 2
    turned = jnp.concatenate([keys[:, half:], keys[:, :half]], axis=1)
    out_ref[:, LAT:] = (keys * cosine_ref[...] + turned * sine_ref[...]).astype(BF16)


def latents(where, hidden, mine, other, gain, cosine, sine):
    tokens, width = hidden.shape
    spec = pltpu.PrefetchScalarGridSpec(
        num_scalar_prefetch=1,
        grid=(1,),
        in_specs=[
            pl.BlockSpec(array.shape, functools.partial(lambda n, i, w: (0,) * n, array.ndim))
            for array in (hidden, mine, other, gain, cosine, sine)
        ],
        out_specs=pl.BlockSpec((tokens, LAT + ROPE), lambda i, w: (0, 0)),
    )
    return call(
        latent_kernel,
        cost=(2 * tokens * width * (LAT + ROPE), 2 * width * (LAT + ROPE)),
        grid_spec=spec,
        out_shape=jax.ShapeDtypeStruct((tokens, LAT + ROPE), BF16),
    )(where, hidden, mine, other, gain, cosine, sine)


def rotation(position):
    freqs = 10000.0 ** (-2.0 * jnp.arange(ROPE // 2, dtype=F32) / ROPE)
    angles = position.astype(F32)[:, None] * freqs[None, :]
    cosine = jnp.cos(angles)
    sine = jnp.sin(angles)
    return jnp.concatenate([cosine, cosine], axis=1), jnp.concatenate([-sine, sine], axis=1)


def pick_kernel(where_ref, whole_ref, part_ref):
    part_ref[...] = whole_ref[...]


def other_groups(where, queries, groups):
    tokens, columns = queries.shape
    block = columns // groups
    spec = pltpu.PrefetchScalarGridSpec(
        num_scalar_prefetch=1,
        grid=(groups // 2,),
        in_specs=[pl.BlockSpec((tokens, block), lambda i, w: (0, 2 * i + 1 - w[0]))],
        out_specs=pl.BlockSpec((tokens, block), lambda i, w: (0, i)),
    )
    return call(
        pick_kernel,
        cost=(0, 2 * tokens * columns),
        grid_spec=spec,
        out_shape=jax.ShapeDtypeStruct((tokens, columns // 2), BF16),
    )(where, queries)


def swap(array):
    return lax.ppermute(array, "c", [(0, 1), (1, 0)])


def along_x(array, distance):
    size = lax.axis_size("x")
    return lax.ppermute(array, "x", [(i, (i + distance) % size) for i in range(size)])


def turn(array, distance, swapped):
    side = lax.axis_size("z")
    pairs = []
    for row in range(side):
        for col in range(side):
            for core in range(2):
                if (core == 0) != swapped:
                    to = ((row + distance) % side, col)
                else:
                    to = (row, (col + distance) % side)
                pairs.append(((row * side + col) * 2 + core, (to[0] * side + to[1]) * 2 + core))
    return lax.ppermute(array, ("z", "y", "c"), pairs)


def ring(block, swapped):
    return [block] + [turn(block, d, swapped) for d in (1, 3, 2)]


def spread(pieces):
    near, right, left, far = pieces
    return jnp.concatenate([near, right, far, left], axis=0)


def exchange(rows):
    return lax.all_to_all(rows, CHIPS, split_axis=0, concat_axis=0, tiled=True)


def shards(
    hidden,
    latent_weight,
    latent_gain,
    queries,
    kv_weight,
    expert_ids,
    route_weights,
    gate_proj,
    up_proj,
    down_proj,
):
    tokens = hidden.shape[0]
    core = lax.axis_index("c")
    chip = lax.axis_index("x")
    chips = lax.axis_size("x")
    nodes = lax.axis_size("z") * lax.axis_size("y")
    where = jnp.stack([core, chip, lax.axis_index("z"), lax.axis_index("y")]).astype(jnp.int32)

    kv_rows, kv_columns = kv_weight.shape
    kv_all = lax.all_gather(kv_weight, CHIPS, axis=0, tiled=True)
    kv_all = kv_all.reshape(nodes, chips, kv_rows, kv_columns)

    slots = nodes * chips * CAP
    rows, gate = dispatch(expert_ids.T, route_weights.T, hidden, slots)

    depth = latent_weight.shape[0] // 2
    part = lax.dynamic_slice_in_dim(latent_weight, core * depth, depth, axis=0)
    pieces = ring(spread(ring(part[None], False)), True)
    own = (gate_proj, up_proj, down_proj)
    pieces, rows, own, queries = lax.optimization_barrier((pieces, rows, own, queries))
    arrived = exchange(rows)
    mine_weight = spread(pieces)
    other = tuple(swap(array) for array in own)
    other_queries = swap(other_groups(where, queries, 2 * chips))

    position = (2 * chip + core) * tokens + jnp.arange(tokens, dtype=jnp.int32)
    cosine, sine = rotation(position)
    mine = latents(
        where, hidden, mine_weight, swap(mine_weight), latent_gain[None], cosine, sine
    )
    pieces = [mine] + [along_x(mine, d) for d in range(1, chips)]

    results = experts(arrived, own, other)
    pieces, results = lax.optimization_barrier((pieces, results))
    line = jnp.concatenate(pieces, axis=0)
    sequence = jnp.concatenate([line, swap(line)], axis=0)
    sequence, results = lax.optimization_barrier((sequence, results))
    returned = exchange(results)

    whole, send = attend(where, sequence, kv_all, queries, other_queries)
    attention = merge(where, swap(send), whole, chips)
    attention, returned = lax.optimization_barrier((attention, returned))
    routed = combine(gate, returned)
    return (attention, routed)


def solution(mesh):
    grid = Mesh(mesh.devices.reshape(4, 4, 4, 2), ALL)
    token = P(ALL, None)
    placed = (
        token,
        P(("z", "y"), None),
        P(),
        token,
        P(("z", "y"), ("x", "c")),
        token,
        token,
        P(ALL, None, None),
        P(ALL, None, None),
        P(ALL, None, None),
    )
    return jax.shard_map(
        shards, mesh=grid, in_specs=placed, out_specs=(token, token), check_vma=False
    )
```

```python
import functools
import math

import jax
import jax.numpy as jnp
from jax import lax
from jax.experimental import pallas as pl
from jax.experimental.pallas import tpu as pltpu
from jax.sharding import Mesh
from jax.sharding import PartitionSpec as P

NOPE = 128
ROPE = 64
VDIM = 128
LAT = 512
EXPERTS = 256
TOPK = 8
CAP = 8
HEAD = NOPE + ROPE
KV = NOPE + VDIM
CHIPS = ("z", "y", "x")
ALL = ("z", "y", "x", "c")
BF16 = jnp.bfloat16
F32 = jnp.float32
MIB = 1 << 20


def call(kernel, **options):
    limit = options.pop("vmem", 32)
    flops, moved = options.pop("cost")
    return pl.pallas_call(
        kernel,
        compiler_params=pltpu.CompilerParams(vmem_limit_bytes=limit * MIB),
        cost_estimate=pl.CostEstimate(flops=flops, bytes_accessed=moved, transcendentals=0),
        **options,
    )


def dispatch_kernel(ids_ref, weights_ref, hidden_ref, rows_ref, gate_ref, pick):
    slots, tokens = pick.shape

    @pl.when(pl.program_id(0) == 0)
    def _():
        row = lax.broadcasted_iota(jnp.int32, (slots, tokens), 0)
        number = (row // CAP) * (EXPERTS * CAP // slots)
        named = jnp.zeros((slots, tokens), F32)
        weight = jnp.zeros((slots, tokens), F32)
        for k in range(TOPK):
            here = ids_ref[k : k + 1, :] == number
            named = jnp.where(here, 1.0, named)
            weight = jnp.where(here, weights_ref[k : k + 1, :], weight)
        before = lax.broadcasted_iota(jnp.int32, (tokens, tokens), 0) < lax.broadcasted_iota(
            jnp.int32, (tokens, tokens), 1
        )
        earlier = jnp.dot(
            named.astype(BF16), before.astype(F32).astype(BF16), preferred_element_type=F32
        )
        kept = (named > 0.5) & (earlier.astype(jnp.int32) == row % CAP)
        pick[...] = jnp.where(kept, 1.0, 0.0).astype(BF16)
        rest = jnp.where(kept, weight, 0.0).T
        for term in range(3):
            part = rest.astype(BF16)
            gate_ref[term * tokens : (term + 1) * tokens, :] = part
            rest = rest - part.astype(F32)

    rows_ref[...] = jnp.dot(pick[...], hidden_ref[...], preferred_element_type=F32).astype(BF16)


def dispatch(ids, weights, hidden, slots):
    tokens, width = hidden.shape
    block = 512
    return call(
        dispatch_kernel,
        cost=(2 * slots * tokens * width, 2 * (slots + tokens) * width),
        grid=(width // block,),
        in_specs=[
            pl.BlockSpec((TOPK, tokens), lambda j: (0, 0)),
            pl.BlockSpec((TOPK, tokens), lambda j: (0, 0)),
            pl.BlockSpec((tokens, block), lambda j: (0, j)),
        ],
        out_specs=[
            pl.BlockSpec((slots, block), lambda j: (0, j)),
            pl.BlockSpec((3 * tokens, slots), lambda j: (0, 0)),
        ],
        out_shape=[
            jax.ShapeDtypeStruct((slots, width), BF16),
            jax.ShapeDtypeStruct((3 * tokens, slots), BF16),
        ],
        scratch_shapes=[pltpu.VMEM((slots, tokens), BF16)],
    )(ids, weights, hidden)


def combine_kernel(gate_ref, rows_ref, out_ref):
    tokens = out_ref.shape[0]
    total = jnp.dot(gate_ref[...], rows_ref[...], preferred_element_type=F32)
    out_ref[...] = (total[:tokens] + total[tokens : 2 * tokens] + total[2 * tokens :]).astype(BF16)


def combine(gate, rows):
    terms, slots = gate.shape
    tokens = terms // 3
    width = rows.shape[1]
    block = 1792
    return call(
        combine_kernel,
        cost=(2 * slots * terms * width, 2 * (slots + tokens) * width),
        grid=(width // block,),
        in_specs=[
            pl.BlockSpec((terms, slots), lambda j: (0, 0)),
            pl.BlockSpec((slots, block), lambda j: (0, j)),
        ],
        out_specs=pl.BlockSpec((tokens, block), lambda j: (0, j)),
        out_shape=jax.ShapeDtypeStruct((tokens, width), BF16),
    )(gate, rows)


def expert_kernel(
    rows_ref, gate0, up0, down0, gate1, up1, down1, out_ref, inner, *, steps
):
    step = pl.program_id(0)

    def hidden_block(gate_ref, up_ref):
        rows = rows_ref[...]
        gate = jnp.dot(rows, gate_ref[0], preferred_element_type=F32)
        upper = jnp.dot(rows, up_ref[0], preferred_element_type=F32)
        inner[step] = (gate / (1.0 + jnp.exp(-gate)) * upper).astype(BF16)

    pl.when(step < steps)(lambda: hidden_block(gate0, up0))
    pl.when((step >= steps) & (step < 2 * steps))(lambda: hidden_block(gate1, up1))

    @pl.when(step >= 2 * steps)
    def _():
        wide = inner.shape[2]
        total = None
        for half, down in enumerate((down0, down1)):
            partial = None
            for part in range(steps):
                term = jnp.dot(
                    inner[half * steps + part],
                    down[0, part * wide : (part + 1) * wide, :],
                    preferred_element_type=F32,
                )
                partial = term if partial is None else partial + term
            partial = partial.astype(BF16).astype(F32)
            total = partial if total is None else total + partial
        out_ref[...] = total.astype(BF16)


def experts(rows, own, other):
    count, width = rows.shape
    half = own[0].shape[2]
    wide, block = 256, 1792
    steps = half // wide
    first = 2 * steps

    def column(start):
        return lambda j: (0, 0, jnp.clip(j - start, 0, steps - 1))

    def late(j):
        return (0, 0, jnp.maximum(j - first, 0))

    specs = []
    for start in (0, steps):
        specs += [
            pl.BlockSpec((1, width, wide), column(start)),
            pl.BlockSpec((1, width, wide), column(start)),
            pl.BlockSpec((1, half, block), late),
        ]
    return call(
        functools.partial(expert_kernel, steps=steps),
        vmem=56,
        cost=(12 * count * width * half, 2 * (2 * count * width + 6 * width * half)),
        grid=(first + width // block,),
        in_specs=[pl.BlockSpec((count, width), lambda j: (0, 0))] + specs,
        out_specs=pl.BlockSpec((count, block), lambda j: (0, jnp.maximum(j - first, 0))),
        out_shape=jax.ShapeDtypeStruct((count, width), BF16),
        scratch_shapes=[pltpu.VMEM((first, count, wide), BF16)],
    )(rows, *own, *other)


def attention_kernel(
    where_ref, latent_ref, kv_ref, mine_ref, other_ref, out_ref, send_ref, bias
):
    tokens = mine_ref.shape[0]
    length = latent_ref.shape[0]
    chips = length // (2 * tokens)

    @pl.when(pl.program_id(0) == 0)
    def _():
        core, chip = where_ref[0], where_ref[1]
        row = lax.broadcasted_iota(jnp.int32, (length, 2 * tokens), 1)
        col = lax.broadcasted_iota(jnp.int32, (length, 2 * tokens), 0)
        row_core = jnp.where(row < tokens, core, 1 - core)
        row_at = (2 * chip + row_core) * tokens + row % tokens
        block = col // tokens
        col_core = jnp.where(block < chips, core, 1 - core)
        col_chip = (chip + chips - block % chips) % chips
        col_at = (2 * col_chip + col_core) * tokens + col % tokens
        bias[...] = jnp.where(col_at <= row_at, 0.0, -1e30)

    compressed = latent_ref[:, :LAT]
    rope = latent_ref[:, LAT:]
    group = kv_ref.shape[3] // KV
    weight = kv_ref[...].reshape(LAT, group * KV)
    keyval = jnp.dot(compressed, weight, preferred_element_type=F32).astype(BF16)
    factor = math.log2(math.e) / math.sqrt(HEAD)
    for head in range(group):
        keys = jnp.concatenate([keyval[:, head * KV : head * KV + NOPE], rope], axis=1)
        values = keyval[:, head * KV + NOPE : (head + 1) * KV]
        span = slice(head * HEAD, (head + 1) * HEAD)
        query = jnp.concatenate([mine_ref[:, span], other_ref[:, span]], axis=0)
        score = lax.dot_general(
            keys, query, (((1,), (1,)), ((), ())), preferred_element_type=F32
        )
        score = score + bias[...]
        top = jnp.max(score, axis=0, keepdims=True)
        weights = jnp.exp2((score - top) * factor)
        inverse = 1.0 / jnp.sum(weights, axis=0, keepdims=True)
        probs = (weights * inverse).astype(BF16)
        result = lax.dot_general(
            probs, values, (((0,), (0,)), ((), ())), preferred_element_type=F32
        ).astype(BF16)
        span = slice(head * VDIM, (head + 1) * VDIM)
        out_ref[:, span] = result[:tokens]
        send_ref[:, span] = result[tokens:]


def attend(where, latent, kv_weight, mine, other):
    tokens = mine.shape[0]
    length = latent.shape[0]
    nodes, chips, rows, columns = kv_weight.shape
    group = columns // KV
    heads = group * chips
    spec = pltpu.PrefetchScalarGridSpec(
        num_scalar_prefetch=1,
        grid=(chips,),
        in_specs=[
            pl.BlockSpec((length, LAT + ROPE), lambda i, w: (0, 0)),
            pl.BlockSpec((nodes, 1, rows, group * KV), lambda i, w: (0, i, 0, 0)),
            pl.BlockSpec(
                (tokens, group * HEAD), lambda i, w: (0, 2 * i + w[0])
            ),
            pl.BlockSpec((tokens, group * HEAD), lambda i, w: (0, i)),
        ],
        out_specs=[
            pl.BlockSpec(
                (tokens, group * VDIM), lambda i, w: (0, 2 * i + w[0])
            ),
            pl.BlockSpec((tokens, group * VDIM), lambda i, w: (0, i)),
        ],
        scratch_shapes=[pltpu.VMEM((length, 2 * tokens), F32)],
    )
    flops = 2 * heads * length * (LAT * KV + 2 * tokens * (HEAD + VDIM))
    return call(
        attention_kernel,
        vmem=48,
        cost=(flops // 4, 2 * (LAT * heads * KV + 4 * tokens * heads * HEAD)),
        grid_spec=spec,
        out_shape=[
            jax.ShapeDtypeStruct((tokens, 2 * heads * VDIM), BF16),
            jax.ShapeDtypeStruct((tokens, heads * VDIM), BF16),
        ],
    )(where, latent, kv_weight, mine, other)


def merge_kernel(where_ref, part_ref, whole_ref, out_ref):
    out_ref[...] = part_ref[...]


def merge(where, part, whole, chips):
    tokens, columns = part.shape
    block = columns // chips
    spec = pltpu.PrefetchScalarGridSpec(
        num_scalar_prefetch=1,
        grid=(chips,),
        in_specs=[
            pl.BlockSpec((tokens, block), lambda i, w: (0, i)),
            pl.BlockSpec(memory_space=pl.ANY),
        ],
        out_specs=pl.BlockSpec((tokens, block), lambda i, w: (0, 2 * i + 1 - w[0])),
    )
    return call(
        merge_kernel,
        cost=(0, 4 * tokens * columns),
        grid_spec=spec,
        out_shape=jax.ShapeDtypeStruct(whole.shape, BF16),
        input_output_aliases={2: 0},
    )(where, part, whole)


def latent_kernel(
    where_ref, hidden_ref, mine_ref, other_ref, gain_ref, cosine_ref, sine_ref, out_ref
):
    core, _, row, col = (where_ref[i] for i in range(4))
    side, blocks, depth = 4, mine_ref.shape[0], mine_ref.shape[1]
    latent = None
    for node in range(blocks):
        by_row = (row + side - node // side) % side
        by_col = (col + side - node % side) % side
        along = by_col * side + by_row
        across = by_row * side + by_col
        start = 2 * depth * node
        lower = hidden_ref[:, start : start + depth]
        upper = hidden_ref[:, start + depth : start + 2 * depth]
        first = core == 0
        for held, block, picked in (
            (mine_ref, jnp.where(first, along, across), jnp.where(first, lower, upper)),
            (other_ref, jnp.where(first, across, along), jnp.where(first, upper, lower)),
        ):
            term = jnp.dot(picked, held[block], preferred_element_type=F32)
            latent = term if latent is None else latent + term
    columns = latent[:, :LAT]
    mean_square = jnp.mean(columns * columns, axis=1, keepdims=True)
    out_ref[:, :LAT] = (columns * lax.rsqrt(mean_square + 1e-06) * gain_ref[...]).astype(BF16)
    keys = latent[:, LAT:]
    half = ROPE // 2
    turned = jnp.concatenate([keys[:, half:], keys[:, :half]], axis=1)
    out_ref[:, LAT:] = (keys * cosine_ref[...] + turned * sine_ref[...]).astype(BF16)


def latents(where, hidden, mine, other, gain, cosine, sine):
    tokens, width = hidden.shape
    spec = pltpu.PrefetchScalarGridSpec(
        num_scalar_prefetch=1,
        grid=(1,),
        in_specs=[
            pl.BlockSpec(array.shape, functools.partial(lambda n, i, w: (0,) * n, array.ndim))
            for array in (hidden, mine, other, gain, cosine, sine)
        ],
        out_specs=pl.BlockSpec((tokens, LAT + ROPE), lambda i, w: (0, 0)),
    )
    return call(
        latent_kernel,
        cost=(2 * tokens * width * (LAT + ROPE), 2 * width * (LAT + ROPE)),
        grid_spec=spec,
        out_shape=jax.ShapeDtypeStruct((tokens, LAT + ROPE), BF16),
    )(where, hidden, mine, other, gain, cosine, sine)


def rotation(position):
    freqs = 10000.0 ** (-2.0 * jnp.arange(ROPE // 2, dtype=F32) / ROPE)
    angles = position.astype(F32)[:, None] * freqs[None, :]
    cosine = jnp.cos(angles)
    sine = jnp.sin(angles)
    return jnp.concatenate([cosine, cosine], axis=1), jnp.concatenate([-sine, sine], axis=1)


def pick_kernel(where_ref, whole_ref, part_ref):
    part_ref[...] = whole_ref[...]


def other_groups(where, queries, groups):
    tokens, columns = queries.shape
    block = columns // groups
    spec = pltpu.PrefetchScalarGridSpec(
        num_scalar_prefetch=1,
        grid=(groups // 2,),
        in_specs=[pl.BlockSpec((tokens, block), lambda i, w: (0, 2 * i + 1 - w[0]))],
        out_specs=pl.BlockSpec((tokens, block), lambda i, w: (0, i)),
    )
    return call(
        pick_kernel,
        cost=(0, 2 * tokens * columns),
        grid_spec=spec,
        out_shape=jax.ShapeDtypeStruct((tokens, columns // 2), BF16),
    )(where, queries)


def swap(array):
    return lax.ppermute(array, "c", [(0, 1), (1, 0)])


def along_x(array, distance):
    size = lax.axis_size("x")
    return lax.ppermute(array, "x", [(i, (i + distance) % size) for i in range(size)])


def turn(array, distance, swapped):
    side = lax.axis_size("z")
    pairs = []
    for row in range(side):
        for col in range(side):
            for core in range(2):
                if (core == 0) != swapped:
                    to = ((row + distance) % side, col)
                else:
                    to = (row, (col + distance) % side)
                pairs.append(((row * side + col) * 2 + core, (to[0] * side + to[1]) * 2 + core))
    return lax.ppermute(array, ("z", "y", "c"), pairs)


def ring(block, swapped):
    return [block] + [turn(block, d, swapped) for d in (1, 3, 2)]


def spread(pieces):
    near, right, left, far = pieces
    return jnp.concatenate([near, right, far, left], axis=0)


def exchange(rows):
    return lax.all_to_all(rows, CHIPS, split_axis=0, concat_axis=0, tiled=True)


def shards(
    hidden,
    latent_weight,
    latent_gain,
    queries,
    kv_weight,
    expert_ids,
    route_weights,
    gate_proj,
    up_proj,
    down_proj,
):
    tokens = hidden.shape[0]
    core = lax.axis_index("c")
    chip = lax.axis_index("x")
    chips = lax.axis_size("x")
    nodes = lax.axis_size("z") * lax.axis_size("y")
    where = jnp.stack([core, chip, lax.axis_index("z"), lax.axis_index("y")]).astype(jnp.int32)

    kv_rows, kv_columns = kv_weight.shape
    kv_all = lax.all_gather(kv_weight, CHIPS, axis=0, tiled=True)
    kv_all = kv_all.reshape(nodes, chips, kv_rows, kv_columns)

    slots = nodes * chips * CAP
    rows, gate = dispatch(expert_ids.T, route_weights.T, hidden, slots)

    depth = latent_weight.shape[0] // 2
    part = lax.dynamic_slice_in_dim(latent_weight, core * depth, depth, axis=0)
    pieces = ring(spread(ring(part[None], False)), True)
    own = (gate_proj, up_proj, down_proj)
    pieces, rows, own, queries = lax.optimization_barrier((pieces, rows, own, queries))
    arrived = exchange(rows)
    mine_weight = spread(pieces)
    other = tuple(swap(array) for array in own)
    other_queries = swap(other_groups(where, queries, 2 * chips))

    position = (2 * chip + core) * tokens + jnp.arange(tokens, dtype=jnp.int32)
    cosine, sine = rotation(position)
    mine = latents(
        where, hidden, mine_weight, swap(mine_weight), latent_gain[None], cosine, sine
    )
    pieces = [mine] + [along_x(mine, d) for d in range(1, chips)]

    results = experts(arrived, own, other)
    pieces, results = lax.optimization_barrier((pieces, results))
    line = jnp.concatenate(pieces, axis=0)
    sequence = jnp.concatenate([line, swap(line)], axis=0)
    sequence, results = lax.optimization_barrier((sequence, results))
    returned = exchange(results)

    whole, send = attend(where, sequence, kv_all, queries, other_queries)
    attention = merge(where, swap(send), whole, chips)
    attention, returned = lax.optimization_barrier((attention, returned))
    routed = combine(gate, returned)
    return (attention, routed)


def solution(mesh):
    grid = Mesh(mesh.devices.reshape(4, 4, 4, 2), ALL)
    token = P(ALL, None)
    placed = (
        token,
        P(("z", "y"), None),
        P(),
        token,
        P(("z", "y"), ("x", "c")),
        token,
        token,
        P(ALL, None, None),
        P(ALL, None, None),
        P(ALL, None, None),
    )
    return jax.shard_map(
        shards, mesh=grid, in_specs=placed, out_specs=(token, token), check_vma=False
    )
```
